32 devices in a mesh: ex: 8 (over y, x, core), ey: 4 (over z).
Axes of the slice: x: 2, y: 2, z: 4, core: 2. Of those that a mesh axis runs over, the one named last changes fastest.
Arguments:
- tokens: bfloat16 [2048, 3584], P(('ex', 'ey')), may hold values from -6 to 6
- route_ids: int32 [2048, 8], P(('ex', 'ey')), may hold values from 0 to 31, all different within a row; in each aligned block of 64 rows (0 to 63, 64 to 127, ...) at most 32 rows name the same one
- route_weight: bfloat16 [2048, 8], P(('ex', 'ey')), may hold values from 0.19921875 to 1
- w_gate: bfloat16 [32, 3584, 1024], P(('ex', 'ey')), may hold values from -0.09375 to 0.09375
- w_up: bfloat16 [32, 3584, 1024], P(('ex', 'ey')), may hold values from -0.09375 to 0.09375
- w_down: bfloat16 [32, 1024, 3584], P(('ex', 'ey')), may hold values from -0.1875 to 0.1875
- shared_gate: bfloat16 [3584, 2048], P(None, 'ex'), may hold values from -0.09375 to 0.09375
- shared_up: bfloat16 [3584, 2048], P(None, 'ex'), may hold values from -0.09375 to 0.09375
- shared_down: bfloat16 [2048, 3584], P('ex'), may hold values from -0.125 to 0.125
Outputs:
- layer_out: bfloat16 [2048, 3584], P(('ex', 'ey'))
The draws below stay inside these ranges and needn't reach their ends.
Inputs may be any that keep to these rules, and one draw needn't show every extreme that they name: `route_ids`: each row names 8 different experts; within the rows of one device no expert is named more than 32 times, a bound that some block reaches.
All inputs are finite; a program needn't handle non-finite values.
Results may differ from the reference program's by a relative error of at most 0.009.
Values may be sent and summed in bfloat16 or wider, within the bound.
No kernel may reach another device: no remote copies, remote signals or barrier semaphores. Data moves between devices by JAX's collectives and lax.ppermute only.
A program may use at most 128 MiB of HBM per device.

```python
import math
import jax
import jax.numpy as jnp
import numpy as np
from jax import lax

D = 3584
FF = 1024
SFF = 2048
TOP = 8
TOK_DEV = 64
EXPERTS = 32
TOKENS = 2048
MOST = 32
N_EX = 8


def block_levels(key, dims, shards, low, largest):
    factor_of = 1.0
    for dim, shards_of in shards:
        draws = jax.random.uniform(jax.random.fold_in(jax.random.fold_in(key, 6), dim), (shards_of,), jnp.float32, low / len(shards), largest / len(shards))
        factor_of = factor_of * jnp.repeat(jnp.exp(draws), dims[dim] // shards_of).reshape((-1,) + (1,) * (len(dims) - 1 - dim))
    return factor_of


def deal_out(own_key, own, number, rows, number_of, top, most, lean):
    sequence = jax.random.permutation(own_key, number_of)
    heavy_load, common = portions_of(number_of, rows * top, most, lean, True), portions_of(number_of, rows * top, most, lean, False)
    places = jnp.arange(number_of)

    def named(lengths, turn):
        used = int((lengths > 0).sum())
        fixed = max(1, used // 4)
        moved = fixed + (places - fixed + turn * (used - fixed)) % max(1, number_of - fixed)
        return jnp.zeros((number_of,), jnp.int32).at[sequence[jnp.where(places < fixed, places, moved)]].set(jnp.asarray(lengths, jnp.int32))

    lengths = jnp.where(number % 4 == 0, named(heavy_load, number // 4), named(common, number - number // 4 - 1))
    mixed = jax.random.permutation(jax.random.fold_in(own, 3), number_of)
    giver, receiver = mixed[0:number_of // 2 * 2:2], mixed[1:number_of // 2 * 2:2]
    slack = jnp.minimum(lengths[giver] - 1, most - lengths[receiver]) // 2
    slack = jnp.where((giver == sequence[0]) | (receiver == sequence[0]) | (lengths[receiver] == 0), 0, jnp.maximum(slack, 0))
    moved = jax.random.randint(jax.random.fold_in(own, 4), (number_of // 2,), 0, 1 << 20) % (slack + 1)
    lengths = lengths.at[giver].add(-moved).at[receiver].add(moved)
    labels = jnp.searchsorted(jnp.cumsum(lengths), jnp.arange(rows * top), side="right").astype(jnp.int32)
    listing = labels.reshape(top, rows).T
    listing = listing[jax.random.permutation(jax.random.fold_in(own, 1), rows)]
    turn = jax.random.randint(jax.random.fold_in(own, 2), (rows, 1), 0, top)
    return jnp.take_along_axis(listing, (jnp.arange(top)[None, :] + turn) % top, axis=1)


def portions_of(number_of, total, most, skew, full):
    loads = [(1 << 20) // math.isqrt(standing ** skew) + 1 for standing in range(1, number_of + 1)]
    largest = most if full else min(most, max(-(-total // number_of), total * loads[0] // sum(loads)))
    least = 1 if total - largest >= number_of - 1 else 0
    holding, surplus = [largest] + [least] * (number_of - 1), total - largest - least * (number_of - 1)
    while surplus > 0:
        candidates = [i for i in range(1, number_of) if holding[i] < largest] or [i for i in range(1, number_of) if holding[i] < most]
        mass, left = sum([loads[i] for i in candidates]), surplus
        for i in candidates:
            addition = min(most - holding[i], max(1, left * loads[i] // mass), surplus)
            holding[i] = holding[i] + addition
            surplus = surplus - addition
    return np.array(holding)


def centred(stream_key, extent, spread, most, cuts=(), kind=jnp.bfloat16):
    array = jax.random.normal(stream_key, extent, jnp.float32) * spread
    if len(cuts) > 0:
        array = block_levels(stream_key, extent, cuts, -0.22, 0.18) * array
    return jnp.clip(array, min=-most, max=most).astype(kind)


def setup_inputs(seed: int = 0) -> dict:
    splits = jax.random.split(jax.random.key(seed), 10)
    tokens = centred(splits[0], (TOKENS, D), 1.0, 6.0, ((0, 32),))
    route_ids_keys = jax.random.split(jax.random.fold_in(splits[1], 1), TOKENS // TOK_DEV)
    route_ids_turns = jax.random.permutation(jax.random.fold_in(splits[1], 3), TOKENS // TOK_DEV)
    route_ids = jax.vmap(lambda own, number: deal_out(jax.random.fold_in(splits[1], 2), own, number, TOK_DEV, EXPERTS, TOP, MOST, 2))(route_ids_keys, route_ids_turns).reshape((TOKENS, TOP))
    route_weight = jnp.clip(jnp.exp(math.log(1.0) - 1.6133518 * jax.random.uniform(splits[2], (TOKENS, TOP), jnp.float32) ** block_levels(splits[2], (TOKENS, TOP), ((0, 32),), -0.2, 0.2)), 0.19921875, 1.0).astype(jnp.bfloat16)
    w_gate = centred(splits[3], (EXPERTS, D, FF), D ** -0.5, 0.09375, ((0, 32),))
    w_up = centred(splits[4], (EXPERTS, D, FF), D ** -0.5, 0.09375, ((0, 32),))
    w_down = centred(splits[5], (EXPERTS, FF, D), FF ** -0.5, 0.1875, ((0, 32),))
    shared_gate = centred(splits[6], (D, SFF), D ** -0.5, 0.09375, ((1, 8),))
    shared_up = centred(splits[7], (D, SFF), D ** -0.5, 0.09375, ((1, 8),))
    shared_down = centred(splits[8], (SFF, D), SFF ** -0.5, 0.125, ((0, 8),))
    return dict(tokens=tokens, route_ids=route_ids, route_weight=route_weight, w_gate=w_gate, w_up=w_up, w_down=w_down, shared_gate=shared_gate, shared_up=shared_up, shared_down=shared_down)


def swiglu(chosen, gate_weight, up_weight, down_weight):
    gate_act = jnp.dot(chosen, gate_weight, preferred_element_type=jnp.float32)
    up_act = jnp.dot(chosen, up_weight, preferred_element_type=jnp.float32)
    hidden = (jax.nn.silu(gate_act) * up_act).astype(jnp.bfloat16)
    return jnp.dot(hidden, down_weight, preferred_element_type=jnp.float32)


def reference(tokens, route_ids, route_weight, w_gate, w_up, w_down, shared_gate, shared_up, shared_down):
    flat_ids = route_ids.reshape(-1).astype(jnp.int32)
    slot_count = TOKENS * TOP
    onehot = (flat_ids[:, None] == jnp.arange(EXPERTS, dtype=jnp.int32)[None, :]).astype(jnp.int32)
    blocks = onehot.reshape(EXPERTS, TOK_DEV * TOP, EXPERTS)
    before = jnp.cumsum(blocks, axis=1) - blocks
    slot_rank = jnp.sum(before * blocks, axis=2).reshape(-1).astype(jnp.int32)
    source = (jnp.arange(slot_count, dtype=jnp.int32) // (TOK_DEV * TOP)).astype(jnp.int32)
    capacity = EXPERTS * MOST
    slot_place = (flat_ids * capacity + source * MOST + slot_rank).astype(jnp.int32)
    token_of = (jnp.arange(slot_count, dtype=jnp.int32) // TOP).astype(jnp.int32)
    lookup = jnp.full((EXPERTS * capacity,), TOKENS, jnp.int32).at[slot_place].set(token_of)
    padded = jnp.concatenate([tokens, jnp.zeros((1, D), tokens.dtype)], axis=0)

    def run_expert(expert):
        picked = lax.dynamic_slice(lookup, (expert * capacity,), (capacity,))
        chosen = padded[picked]
        return swiglu(chosen, w_gate[expert], w_up[expert], w_down[expert]).astype(jnp.bfloat16)

    results = lax.map(run_expert, jnp.arange(EXPERTS, dtype=jnp.int32))
    slot_out = results.reshape(-1, D)[slot_place]
    weighted = slot_out.astype(jnp.float32).reshape(TOKENS, TOP, D) * route_weight.astype(jnp.float32)[:, :, None]
    routed = jnp.sum(weighted, axis=1)
    group = SFF // N_EX
    shared = jnp.zeros((TOKENS, D), jnp.float32)
    for index in range(N_EX):
        low = index * group
        part_value = swiglu(tokens, shared_gate[:, low:low + group], shared_up[:, low:low + group], shared_down[low:low + group, :])
        shared = shared + part_value.astype(jnp.bfloat16).astype(jnp.float32)
    return (shared + routed).astype(jnp.bfloat16)
```

```python
import jax
import jax.numpy as jnp
from jax import lax
from jax.sharding import PartitionSpec as P


def swiglu(chosen, gate_weight, up_weight, down_weight):
    gate_act = jnp.dot(chosen, gate_weight, preferred_element_type=jnp.float32)
    up_act = jnp.dot(chosen, up_weight, preferred_element_type=jnp.float32)
    hidden = (jax.nn.silu(gate_act) * up_act).astype(jnp.bfloat16)
    return jnp.dot(hidden, down_weight, preferred_element_type=jnp.float32)


def shared_expert(tokens, shared_gate, shared_up, shared_down):
    gathered = lax.all_gather(tokens, "ex", axis=0, tiled=True)
    return lax.psum_scatter(
        swiglu(gathered, shared_gate, shared_up, shared_down).astype(jnp.bfloat16),
        "ex",
        scatter_dimension=0,
        tiled=True,
    ).astype(jnp.float32)


def exchange_slots(
    tokens, route_ids, route_weight, w_gate, w_up, w_down, shared_gate, shared_up, shared_down
):
    tok_rows = tokens.shape[0]
    top_count = route_ids.shape[1]
    width = tokens.shape[1]
    experts = lax.axis_size("ex") * lax.axis_size("ey")
    slot_most = max(2, 2 * tok_rows * top_count // experts)
    capacity = experts * slot_most
    flat_ids = route_ids.reshape(-1)
    onehot = (flat_ids[:, None] == jnp.arange(experts, dtype=jnp.int32)[None, :]).astype(jnp.int32)
    slot_rank = jnp.sum((jnp.cumsum(onehot, axis=0) - onehot) * onehot, axis=1)
    slot_place = flat_ids * slot_most + slot_rank
    matches = (slot_place[:, None] == jnp.arange(capacity, dtype=jnp.int32)[None, :]).astype(
        jnp.float32
    )
    matches = matches.reshape(tok_rows, top_count, capacity)
    placing = jnp.sum(matches, axis=1).astype(jnp.bfloat16)
    combine_mat = jnp.sum(matches * route_weight.astype(jnp.float32)[:, :, None], axis=1).astype(
        jnp.bfloat16
    )
    outgoing = jnp.einsum("tc,td->cd", placing, tokens, preferred_element_type=jnp.float32).astype(
        jnp.bfloat16
    )
    outgoing = outgoing.reshape(experts, slot_most, width)
    arrived = lax.all_to_all(outgoing, ("ex", "ey"), split_axis=0, concat_axis=0, tiled=True)
    layout = arrived.shape
    result = swiglu(arrived.reshape(-1, width), w_gate[0], w_up[0], w_down[0])
    produced = result.astype(jnp.bfloat16).reshape(layout)
    returned = lax.all_to_all(produced, ("ex", "ey"), split_axis=0, concat_axis=0, tiled=True)
    returned = returned.reshape(capacity, width)
    routed = jnp.dot(combine_mat, returned, preferred_element_type=jnp.float32)
    shared = shared_expert(tokens, shared_gate, shared_up, shared_down)
    return (shared + routed).astype(jnp.bfloat16)


PAIR, RIGHT, DOWN = 1, 2, 4


def swap(value, axis, mask):
    size = lax.axis_size(axis)
    return lax.ppermute(value, axis, [(i, i ^ mask) for i in range(size)])


def gather_plane(own):
    rows = own.shape[0]
    half = rows // 2
    right = swap(own, "ex", RIGHT)
    down = swap(own, "ex", DOWN)
    across_low = swap(right[:half], "ex", DOWN)
    across_high = swap(down[half:], "ex", RIGHT)
    mine = jnp.concatenate([own, right, down, across_low, across_high], axis=0)
    other = swap(mine, "ex", PAIR)
    return mine, other


def reduce_plane(mine, other):
    rows = mine.shape[0] // 4
    half = rows // 2
    f32 = jnp.float32
    got = swap(other, "ex", PAIR)

    def pair_sum(low, high):
        return mine[low:high].astype(f32) + got[low:high].astype(f32)

    across = pair_sum(3 * rows, 4 * rows).astype(jnp.bfloat16)
    from_down = swap(across[:half], "ex", DOWN)
    from_right = swap(across[half:], "ex", RIGHT)
    zero = jnp.zeros((half, mine.shape[1]), f32)
    right = pair_sum(rows, 2 * rows) + jnp.concatenate([from_down.astype(f32), zero], axis=0)
    down = pair_sum(2 * rows, 3 * rows) + jnp.concatenate([zero, from_right.astype(f32)], axis=0)
    got_right = swap(right.astype(jnp.bfloat16), "ex", RIGHT)
    got_down = swap(down.astype(jnp.bfloat16), "ex", DOWN)
    return pair_sum(0, rows) + got_right.astype(f32) + got_down.astype(f32)


def run_expert(pieces, width, block, most, weights):
    top = (pieces.shape[1] - width) // 2
    tokens = pieces[:, :width].reshape(-1, block, width)
    ids = pieces[:, width : width + top]
    rates = pieces[:, width + top :]
    me = lax.axis_index("ex") * lax.axis_size("ey") + lax.axis_index("ey")
    hit = ids == me.astype(jnp.bfloat16)
    rate = jnp.sum(jnp.where(hit, rates, 0).astype(jnp.float32), axis=1).reshape(-1, block)
    named = jnp.any(hit, axis=1).reshape(-1, block)
    before = jnp.tril(jnp.ones((block, block), jnp.bfloat16), -1)
    rank = jnp.einsum(
        "nt,st->ns", named.astype(jnp.bfloat16), before, preferred_element_type=jnp.float32
    ).astype(jnp.int32)
    place = (rank[:, None, :] == jnp.arange(most, dtype=jnp.int32)[None, :, None]) & named[:, None]
    chosen = jnp.einsum(
        "nct,ntd->ncd", place.astype(jnp.bfloat16), tokens, preferred_element_type=jnp.float32
    ).astype(jnp.bfloat16)
    out = swiglu(chosen.reshape(-1, width), *weights).astype(jnp.bfloat16)
    combine = jnp.where(place, rate[:, None, :], 0).astype(jnp.bfloat16)
    back = jnp.einsum(
        "nct,ncd->ntd",
        combine,
        out.reshape(-1, most, width),
        preferred_element_type=jnp.float32,
    )
    return back.reshape(-1, width)


def gather_all(
    tokens, route_ids, route_weight, w_gate, w_up, w_down, shared_gate, shared_up, shared_down
):
    block, width = tokens.shape
    planes = lax.axis_size("ey")
    experts = lax.axis_size("ex") * planes
    most = max(2, 2 * block * route_ids.shape[1] // experts)
    weights = (w_gate[0], w_up[0], w_down[0])
    own = jnp.concatenate([tokens, route_ids.astype(jnp.bfloat16), route_weight], axis=1)
    columns = [own] + [swap(own, "ey", mask) for mask in range(1, planes)]
    total = None
    sums = []
    for mask in list(range(1, planes)) + [0]:
        mine, other = gather_plane(columns[mask])
        mine_out = run_expert(mine, width, block, most, weights)
        other_out = run_expert(other, width, block, most, weights)
        if mask == 0:
            mine_out += swiglu(mine[:, :width], shared_gate, shared_up, shared_down)
            other_out += swiglu(other[:, :width], shared_gate, shared_up, shared_down)
        part = reduce_plane(mine_out.astype(jnp.bfloat16), other_out.astype(jnp.bfloat16))
        if mask:
            part = swap(part.astype(jnp.bfloat16), "ey", mask).astype(jnp.float32)
        sums.append(part)
    total = sums[0]
    for part in sums[1:]:
        total = total + part
    return total.astype(jnp.bfloat16)


def solution(mesh):
    sizes = dict(mesh.shape)

    def shards(*args):
        tokens, route_ids = args[0], args[1]
        slots = max(2, 2 * tokens.shape[0] * route_ids.shape[1] // (sizes["ex"] * sizes["ey"]))
        cube = sizes["ex"] == 2 * DOWN and sizes["ey"] & (sizes["ey"] - 1) == 0
        if cube and 4 * slots > tokens.shape[0]:
            return gather_all(*args)
        return exchange_slots(*args)

    in_specs = (
        P(("ex", "ey"), None),
        P(("ex", "ey"), None),
        P(("ex", "ey"), None),
        P(("ex", "ey"), None, None),
        P(("ex", "ey"), None, None),
        P(("ex", "ey"), None, None),
        P(None, "ex"),
        P(None, "ex"),
        P("ex", None),
    )
    out_specs = P(("ex", "ey"), None)
    return jax.shard_map(shards, mesh=mesh, in_specs=in_specs, out_specs=out_specs, check_vma=False)
```

```python
import functools

import jax
import jax.numpy as jnp
from jax import lax
from jax.experimental import pallas as pl
from jax.experimental.pallas import tpu as pltpu
from jax.sharding import PartitionSpec as P


def swiglu(chosen, gate_weight, up_weight, down_weight):
    gate_act = jnp.dot(chosen, gate_weight, preferred_element_type=jnp.float32)
    up_act = jnp.dot(chosen, up_weight, preferred_element_type=jnp.float32)
    hidden = (jax.nn.silu(gate_act) * up_act).astype(jnp.bfloat16)
    return jnp.dot(hidden, down_weight, preferred_element_type=jnp.float32)


def shared_expert(tokens, shared_gate, shared_up, shared_down):
    gathered = lax.all_gather(tokens, "ex", axis=0, tiled=True)
    return lax.psum_scatter(
        swiglu(gathered, shared_gate, shared_up, shared_down).astype(jnp.bfloat16),
        "ex",
        scatter_dimension=0,
        tiled=True,
    ).astype(jnp.float32)


def exchange_slots(
    tokens, route_ids, route_weight, w_gate, w_up, w_down, shared_gate, shared_up, shared_down
):
    tok_rows = tokens.shape[0]
    top_count = route_ids.shape[1]
    width = tokens.shape[1]
    experts = lax.axis_size("ex") * lax.axis_size("ey")
    slot_most = max(2, 2 * tok_rows * top_count // experts)
    capacity = experts * slot_most
    flat_ids = route_ids.reshape(-1)
    onehot = (flat_ids[:, None] == jnp.arange(experts, dtype=jnp.int32)[None, :]).astype(jnp.int32)
    slot_rank = jnp.sum((jnp.cumsum(onehot, axis=0) - onehot) * onehot, axis=1)
    slot_place = flat_ids * slot_most + slot_rank
    matches = (slot_place[:, None] == jnp.arange(capacity, dtype=jnp.int32)[None, :]).astype(
        jnp.float32
    )
    matches = matches.reshape(tok_rows, top_count, capacity)
    placing = jnp.sum(matches, axis=1).astype(jnp.bfloat16)
    combine_mat = jnp.sum(matches * route_weight.astype(jnp.float32)[:, :, None], axis=1).astype(
        jnp.bfloat16
    )
    outgoing = jnp.einsum("tc,td->cd", placing, tokens, preferred_element_type=jnp.float32).astype(
        jnp.bfloat16
    )
    outgoing = outgoing.reshape(experts, slot_most, width)
    arrived = lax.all_to_all(outgoing, ("ex", "ey"), split_axis=0, concat_axis=0, tiled=True)
    layout = arrived.shape
    result = swiglu(arrived.reshape(-1, width), w_gate[0], w_up[0], w_down[0])
    produced = result.astype(jnp.bfloat16).reshape(layout)
    returned = lax.all_to_all(produced, ("ex", "ey"), split_axis=0, concat_axis=0, tiled=True)
    returned = returned.reshape(capacity, width)
    routed = jnp.dot(combine_mat, returned, preferred_element_type=jnp.float32)
    shared = shared_expert(tokens, shared_gate, shared_up, shared_down)
    return (shared + routed).astype(jnp.bfloat16)


PAIR, RIGHT, DOWN = 1, 2, 4


def swap(value, axis, mask):
    size = lax.axis_size(axis)
    return lax.ppermute(value, axis, [(i, i ^ mask) for i in range(size)])


def gather_plane(own, turn):
    right = swap(own, "ex", RIGHT)
    down = swap(own, "ex", DOWN)
    across = swap(down, "ex", RIGHT) if turn else swap(right, "ex", DOWN)
    return [own, right, down, across]


def reduce_plane(mine, other, turn):
    rows = mine.shape[0] // 4
    f32 = jnp.float32
    got = swap(other, "ex", PAIR)

    def pair_sum(piece):
        low = piece * rows
        return mine[low : low + rows].astype(f32) + got[low : low + rows].astype(f32)

    across = swap(pair_sum(3).astype(jnp.bfloat16), "ex", RIGHT if turn else DOWN).astype(f32)
    right, down = pair_sum(1), pair_sum(2)
    if turn:
        down = down + across
    else:
        right = right + across
    got_right = swap(right.astype(jnp.bfloat16), "ex", RIGHT)
    got_down = swap(down.astype(jnp.bfloat16), "ex", DOWN)
    return pair_sum(0) + got_right.astype(f32) + got_down.astype(f32)


LANES = 128


def tile_of(size, goal):
    return max(t for t in range(LANES, goal + 1, LANES) if size % t == 0)


def expert_body(dims, *refs):
    count, block, most, width, hidden, shared_hidden, tile, span = dims
    rows, slots = count * block, count * most
    refs = list(refs)

    def take(number):
        out = refs[:number]
        del refs[:number]
        return out

    pieces = take(2 * count)
    w_gate, w_up, w_down = take(3)
    shared = take(3) if shared_hidden else None
    outs = take(2)
    held, chosen, gate, up, down, act, back, result = take(8)
    if shared:
        s_gate, s_up, s_down, s_act = take(4)
    piece_sem, gate_sem, up_sem, down_sem, out_sem = take(5)
    if shared:
        (shared_sem,) = take(1)
    copy = pltpu.make_async_copy
    steps, spans = hidden // tile, width // span
    f32, bf16 = jnp.float32, jnp.bfloat16

    def piece_copy(k):
        return copy(pieces[k], held.at[pl.ds(k * block, block), :], piece_sem.at[k])

    def gate_copy(k):
        return copy(w_gate.at[0, :, pl.ds(k * tile, tile)], gate.at[k], gate_sem.at[k])

    def up_copy(k):
        return copy(w_up.at[0, :, pl.ds(k * tile, tile)], up.at[k], up_sem.at[k])

    def down_copy(k):
        return copy(w_down.at[0, :, pl.ds(k * span, span)], down.at[k], down_sem.at[k])

    def shared_copy(k):
        return copy(shared[k], (s_gate, s_up, s_down)[k], shared_sem.at[k])

    def out_copy(side, k):
        return copy(
            result.at[side, k], outs[side].at[:, pl.ds(k * span, span)], out_sem.at[side, k]
        )

    for k in range(2 * count):
        piece_copy(k).start()
    if shared:
        shared_copy(0).start()
        shared_copy(1).start()
    for k in range(steps):
        gate_copy(k).start()
        up_copy(k).start()
    if shared:
        shared_copy(2).start()
    for k in range(spans):
        down_copy(k).start()

    me = lax.axis_index("ex") * lax.axis_size("ey") + lax.axis_index("ey")
    pick = (lax.broadcasted_iota(jnp.int32, (16, LANES), 1) == me).astype(f32).astype(bf16)
    early = lax.broadcasted_iota(jnp.int32, (rows, rows), 0)
    late = lax.broadcasted_iota(jnp.int32, (rows, rows), 1)
    before = ((early < late) & (early // block == late // block)).astype(f32).astype(bf16)
    base = (lax.broadcasted_iota(jnp.int32, (1, rows), 1) // block * most).astype(f32)
    slot = lax.broadcasted_iota(jnp.int32, (slots, rows), 0).astype(f32)
    for side in range(2):
        for k in range(side * count, (side + 1) * count):
            piece_copy(k).wait()
        low = side * rows
        table = held[low : low + rows, width : width + LANES]
        rate = lax.dot_general(
            pick, table, (((1,), (1,)), ((), ())), preferred_element_type=f32
        )
        named = (rate > 0).astype(f32)
        rank = jnp.dot(named.astype(bf16), before, preferred_element_type=f32)
        where = jnp.where(named[0:1] > 0, rank[0:1] + base, -1.0)
        place = slot == where
        back[side] = jnp.where(place, rate[0:1], 0.0).T.astype(bf16)
        onehot = place.astype(f32).astype(bf16)

        @pl.loop(0, spans)
        def _(k):
            columns = pl.ds(pl.multiple_of(k * span, span), span)
            chosen[side * slots : (side + 1) * slots, columns] = jnp.dot(
                onehot, held[low : low + rows, columns], preferred_element_type=f32
            ).astype(bf16)

    if shared:
        shared_copy(0).wait()
        shared_copy(1).wait()
        tokens = held[:, :width]
        g = jnp.dot(tokens, s_gate[...], preferred_element_type=f32)
        u = jnp.dot(tokens, s_up[...], preferred_element_type=f32)
        s_act[...] = (jax.nn.silu(g) * u).astype(bf16)

    @pl.loop(0, steps)
    def _(k):
        gate_copy(k).wait()
        up_copy(k).wait()
        g = jnp.dot(chosen[...], gate[k], preferred_element_type=f32)
        u = jnp.dot(chosen[...], up[k], preferred_element_type=f32)
        act[:, pl.ds(pl.multiple_of(k * tile, tile), tile)] = (jax.nn.silu(g) * u).astype(bf16)

    if shared:
        shared_copy(2).wait()

    @pl.loop(0, spans)
    def _(k):
        down_copy(k).wait()
        y = jnp.dot(act[...], down[k], preferred_element_type=f32).astype(bf16)
        for side in (1, 0):
            out = jnp.dot(
                back[side], y[side * slots : (side + 1) * slots], preferred_element_type=f32
            )
            if shared:
                out += jnp.dot(
                    s_act[side * rows : (side + 1) * rows],
                    s_down[:, pl.ds(pl.multiple_of(k * span, span), span)],
                    preferred_element_type=f32,
                )
            result[side, k] = out.astype(bf16)
            out_copy(side, k).start()

    for k in range(spans):
        out_copy(0, k).wait()
        out_copy(1, k).wait()


def run_expert(mine, other, most, weights, shared):
    count, (block, wide) = len(mine), mine[0].shape
    width, hidden = wide - LANES, weights[0].shape[2]
    shared_hidden = shared[0].shape[1] if shared else 0
    tile, span = tile_of(hidden, 256), tile_of(width, 1024)
    rows, slots = count * block, count * most
    dims = (count, block, most, width, hidden, shared_hidden, tile, span)
    bf16 = jnp.bfloat16
    vmem, sems = pltpu.VMEM, pltpu.SemaphoreType.DMA
    scratch = [
        vmem((2 * rows, wide), bf16),
        vmem((2 * slots, width), bf16),
        vmem((hidden // tile, width, tile), bf16),
        vmem((hidden // tile, width, tile), bf16),
        vmem((width // span, hidden, span), bf16),
        vmem((2 * slots, hidden), bf16),
        vmem((2, rows, slots), bf16),
        vmem((2, width // span, rows, span), bf16),
    ]
    if shared:
        scratch += [vmem(part.shape, bf16) for part in shared]
        scratch += [vmem((2 * rows, shared_hidden), bf16)]
    scratch += [
        sems((2 * count,)),
        sems((hidden // tile,)),
        sems((hidden // tile,)),
        sems((width // span,)),
        sems((2, width // span)),
    ]
    if shared:
        scratch += [sems((3,))]
    operands = [*mine, *other, *weights, *(shared or ())]
    flops = 2 * (6 * slots * width * hidden + 4 * rows * slots * width)
    flops += 2 * 6 * rows * width * shared_hidden
    moved = 2 * (sum(part.size for part in operands) + 2 * rows * width)
    return pl.pallas_call(
        functools.partial(expert_body, dims),
        out_shape=[jax.ShapeDtypeStruct((rows, width), bf16)] * 2,
        in_specs=[pl.BlockSpec(memory_space=pl.ANY)] * len(operands),
        out_specs=[pl.BlockSpec(memory_space=pl.ANY)] * 2,
        scratch_shapes=scratch,
        compiler_params=pltpu.CompilerParams(vmem_limit_bytes=52 * 1024 * 1024),
        cost_estimate=pl.CostEstimate(flops=flops, bytes_accessed=moved, transcendentals=0),
    )(*operands)


def gather_all(
    tokens, route_ids, route_weight, w_gate, w_up, w_down, shared_gate, shared_up, shared_down
):
    block = tokens.shape[0]
    planes = lax.axis_size("ey")
    experts = lax.axis_size("ex") * planes
    most = max(2, 2 * block * route_ids.shape[1] // experts)
    hit = route_ids[:, :, None] == jnp.arange(LANES, dtype=jnp.int32)
    table = jnp.sum(jnp.where(hit, route_weight[:, :, None], 0).astype(jnp.float32), axis=1)
    own = jnp.concatenate([tokens, table.astype(tokens.dtype)], axis=1)
    columns = [own] + [swap(own, "ey", mask) for mask in range(1, planes)]
    order = list(range(1, planes)) + [0]
    sums = []
    for mask in order:
        mine = gather_plane(columns[mask], mask % 2)
        other = [swap(piece, "ex", PAIR) for piece in mine]
        shared = None if mask else (shared_gate, shared_up, shared_down)
        mine, other = run_expert(mine, other, most, (w_gate, w_up, w_down), shared)
        part = reduce_plane(mine, other, mask % 2)
        if mask:
            part = swap(part.astype(jnp.bfloat16), "ey", mask).astype(jnp.float32)
        sums.append(part)
    total = sums[0]
    for part in sums[1:]:
        total = total + part
    return total.astype(jnp.bfloat16)


def solution(mesh):
    sizes = dict(mesh.shape)

    def shards(*args):
        tokens, route_ids = args[0], args[1]
        slots = max(2, 2 * tokens.shape[0] * route_ids.shape[1] // (sizes["ex"] * sizes["ey"]))
        cube = sizes["ex"] == 2 * DOWN and sizes["ey"] & (sizes["ey"] - 1) == 0
        cube = cube and sizes["ex"] * sizes["ey"] <= LANES
        if cube and 4 * slots > tokens.shape[0]:
            return gather_all(*args)
        return exchange_slots(*args)

    in_specs = (
        P(("ex", "ey"), None),
        P(("ex", "ey"), None),
        P(("ex", "ey"), None),
        P(("ex", "ey"), None, None),
        P(("ex", "ey"), None, None),
        P(("ex", "ey"), None, None),
        P(None, "ex"),
        P(None, "ex"),
        P("ex", None),
    )
    out_specs = P(("ex", "ey"), None)
    return jax.shard_map(shards, mesh=mesh, in_specs=in_specs, out_specs=out_specs, check_vma=False)
```

```python
import functools

import jax
import jax.numpy as jnp
import numpy as np
from jax import lax
from jax.experimental import pallas as pl
from jax.experimental.pallas import tpu as pltpu
from jax.sharding import PartitionSpec as P


def swiglu(chosen, gate_weight, up_weight, down_weight):
    gate_act = jnp.dot(chosen, gate_weight, preferred_element_type=jnp.float32)
    up_act = jnp.dot(chosen, up_weight, preferred_element_type=jnp.float32)
    hidden = (jax.nn.silu(gate_act) * up_act).astype(jnp.bfloat16)
    return jnp.dot(hidden, down_weight, preferred_element_type=jnp.float32)


def shared_expert(tokens, shared_gate, shared_up, shared_down):
    gathered = lax.all_gather(tokens, "ex", axis=0, tiled=True)
    return lax.psum_scatter(
        swiglu(gathered, shared_gate, shared_up, shared_down).astype(jnp.bfloat16),
        "ex",
        scatter_dimension=0,
        tiled=True,
    ).astype(jnp.float32)


def exchange_slots(
    tokens, route_ids, route_weight, w_gate, w_up, w_down, shared_gate, shared_up, shared_down
):
    tok_rows = tokens.shape[0]
    top_count = route_ids.shape[1]
    width = tokens.shape[1]
    experts = lax.axis_size("ex") * lax.axis_size("ey")
    slot_most = max(2, 2 * tok_rows * top_count // experts)
    capacity = experts * slot_most
    flat_ids = route_ids.reshape(-1)
    onehot = (flat_ids[:, None] == jnp.arange(experts, dtype=jnp.int32)[None, :]).astype(jnp.int32)
    slot_rank = jnp.sum((jnp.cumsum(onehot, axis=0) - onehot) * onehot, axis=1)
    slot_place = flat_ids * slot_most + slot_rank
    matches = (slot_place[:, None] == jnp.arange(capacity, dtype=jnp.int32)[None, :]).astype(
        jnp.float32
    )
    matches = matches.reshape(tok_rows, top_count, capacity)
    placing = jnp.sum(matches, axis=1).astype(jnp.bfloat16)
    combine_mat = jnp.sum(matches * route_weight.astype(jnp.float32)[:, :, None], axis=1).astype(
        jnp.bfloat16
    )
    outgoing = jnp.einsum("tc,td->cd", placing, tokens, preferred_element_type=jnp.float32).astype(
        jnp.bfloat16
    )
    outgoing = outgoing.reshape(experts, slot_most, width)
    arrived = lax.all_to_all(outgoing, ("ex", "ey"), split_axis=0, concat_axis=0, tiled=True)
    layout = arrived.shape
    result = swiglu(arrived.reshape(-1, width), w_gate[0], w_up[0], w_down[0])
    produced = result.astype(jnp.bfloat16).reshape(layout)
    returned = lax.all_to_all(produced, ("ex", "ey"), split_axis=0, concat_axis=0, tiled=True)
    returned = returned.reshape(capacity, width)
    routed = jnp.dot(combine_mat, returned, preferred_element_type=jnp.float32)
    shared = shared_expert(tokens, shared_gate, shared_up, shared_down)
    return (shared + routed).astype(jnp.bfloat16)


PAIR, RIGHT, DOWN = 1, 2, 4


def swap(value, axis, mask):
    size = lax.axis_size(axis)
    return lax.ppermute(value, axis, [(i, i ^ mask) for i in range(size)])


def gather_plane(own, turn):
    right = swap(own, "ex", RIGHT)
    down = swap(own, "ex", DOWN)
    across = swap(down, "ex", RIGHT) if turn else swap(right, "ex", DOWN)
    return [own, right, down, across]


def add_body(jobs, *refs):
    outs = refs[len(refs) - len(jobs) :]
    at = 0
    for out, job in zip(outs, jobs):
        total = refs[at][...].astype(jnp.float32)
        for k in range(1, job):
            total += refs[at + k][...].astype(jnp.float32)
        out[...] = total.astype(out.dtype)
        at += job


def add_rows(rows, jobs):
    width = jobs[0][0][0].shape[1]
    steps = 2
    span = width // steps

    def spec(block):
        return pl.BlockSpec((rows, span), lambda j: (block, j))

    return pl.pallas_call(
        functools.partial(add_body, tuple(len(job) for job in jobs)),
        grid=(steps,),
        out_shape=[jax.ShapeDtypeStruct((rows, width), jnp.bfloat16)] * len(jobs),
        in_specs=[spec(block) for job in jobs for _, block in job],
        out_specs=[spec(0)] * len(jobs),
        cost_estimate=pl.CostEstimate(
            flops=sum(map(len, jobs)) * rows * width,
            bytes_accessed=2 * (sum(map(len, jobs)) + len(jobs)) * rows * width,
            transcendentals=0,
        ),
    )(*[array for job in jobs for array, _ in job])


LANES = 128


def tile_of(size, goal):
    return max(t for t in range(LANES, goal + 1, LANES) if size % t == 0)


def expert_body(dims, trailing, *refs):
    count, block, most, width, hidden, shared_hidden, tile, span = dims
    rows, slots = count * block, count * most
    refs = list(refs)

    def take(number):
        out = refs[:number]
        del refs[:number]
        return out

    pieces = take(2 * count)
    (before_ref,) = take(1)
    w_gate, w_up, w_down = take(3)
    shared = take(3) if shared_hidden else None
    take(len(refs) - trailing)
    outs = take(2)
    held, chosen, gate, up, down, act, back, result = take(8)
    if shared:
        s_gate, s_up, s_down, s_act = take(4)
    piece_sem, gate_sem, up_sem, down_sem, out_sem = take(5)
    if shared:
        (shared_sem,) = take(1)
    copy = pltpu.make_async_copy
    steps, spans = hidden // tile, width // span
    f32, bf16 = jnp.float32, jnp.bfloat16

    def piece_copy(k):
        return copy(pieces[k], held.at[pl.ds(k * block, block), :], piece_sem.at[k])

    def gate_copy(k):
        return copy(w_gate.at[0, :, pl.ds(k * tile, tile)], gate.at[k], gate_sem.at[k])

    def up_copy(k):
        return copy(w_up.at[0, :, pl.ds(k * tile, tile)], up.at[k], up_sem.at[k])

    def down_copy(k):
        return copy(w_down.at[0, :, pl.ds(k * span, span)], down.at[k], down_sem.at[k])

    def shared_copy(k):
        return copy(shared[k], (s_gate, s_up, s_down)[k], shared_sem.at[k])

    def out_copy(side, k):
        return copy(
            result.at[side, k], outs[side].at[:, pl.ds(k * span, span)], out_sem.at[side, k]
        )

    for k in range(2 * count):
        piece_copy(k).start()
    if shared:
        shared_copy(0).start()
        shared_copy(1).start()

    me = lax.axis_index("ex") * lax.axis_size("ey") + lax.axis_index("ey")
    pick = (lax.broadcasted_iota(jnp.int32, (16, LANES), 1) == me).astype(f32).astype(bf16)
    before = before_ref[:rows]
    base = before_ref[rows : rows + 16].astype(f32)[0:1]
    slot = lax.broadcasted_iota(jnp.int32, (slots, rows), 0).astype(f32)
    for side in range(2):
        for k in range(side * count, (side + 1) * count):
            piece_copy(k).wait()
        if side == 1:
            for k in range(steps):
                gate_copy(k).start()
                up_copy(k).start()
            if shared:
                shared_copy(2).start()
            for k in range(spans):
                down_copy(k).start()
        low = side * rows
        table = held[low : low + rows, width : width + LANES]
        rate = lax.dot_general(
            pick, table, (((1,), (1,)), ((), ())), preferred_element_type=f32
        )
        named = (rate > 0).astype(f32)
        rank = jnp.dot(named.astype(bf16), before, preferred_element_type=f32)
        where = jnp.where(named[0:1] > 0, rank[0:1] + base, -1.0)
        place = slot == where
        back[side] = jnp.where(place, rate[0:1], 0.0).T.astype(bf16)
        onehot = place.astype(f32).astype(bf16)

        chosen[side * slots : (side + 1) * slots] = jnp.dot(
            onehot, held[low : low + rows, :width], preferred_element_type=f32
        ).astype(bf16)

    if shared:
        shared_copy(0).wait()
        shared_copy(1).wait()
        tokens = held[:, :width]
        g = jnp.dot(tokens, s_gate[...], preferred_element_type=f32)
        u = jnp.dot(tokens, s_up[...], preferred_element_type=f32)
        s_act[...] = (jax.nn.silu(g) * u).astype(bf16)

    @pl.loop(0, steps)
    def _(k):
        gate_copy(k).wait()
        up_copy(k).wait()
        g = jnp.dot(chosen[...], gate[k], preferred_element_type=f32)
        u = jnp.dot(chosen[...], up[k], preferred_element_type=f32)
        act[:, pl.ds(pl.multiple_of(k * tile, tile), tile)] = (jax.nn.silu(g) * u).astype(bf16)

    if shared:
        shared_copy(2).wait()

    @pl.loop(0, spans)
    def _(k):
        down_copy(k).wait()
        y = jnp.dot(act[...], down[k], preferred_element_type=f32).astype(bf16)
        for side in (1, 0):
            out = jnp.dot(
                back[side], y[side * slots : (side + 1) * slots], preferred_element_type=f32
            )
            if shared:
                out += jnp.dot(
                    s_act[side * rows : (side + 1) * rows],
                    s_down[:, pl.ds(pl.multiple_of(k * span, span), span)],
                    preferred_element_type=f32,
                )
            result[side, k] = out.astype(bf16)
            out_copy(side, k).start()

    for k in range(spans):
        out_copy(0, k).wait()
        out_copy(1, k).wait()


def run_expert(mine, other, most, weights, shared, after=()):
    count, (block, wide) = len(mine), mine[0].shape
    width, hidden = wide - LANES, weights[0].shape[2]
    shared_hidden = shared[0].shape[1] if shared else 0
    tile, span = tile_of(hidden, 256), tile_of(width, 1024)
    rows, slots = count * block, count * most
    dims = (count, block, most, width, hidden, shared_hidden, tile, span)
    bf16 = jnp.bfloat16
    vmem, sems = pltpu.VMEM, pltpu.SemaphoreType.DMA
    scratch = [
        vmem((2 * rows, wide), bf16),
        vmem((2 * slots, width), bf16),
        vmem((hidden // tile, width, tile), bf16),
        vmem((hidden // tile, width, tile), bf16),
        vmem((width // span, hidden, span), bf16),
        vmem((2 * slots, hidden), bf16),
        vmem((2, rows, slots), bf16),
        vmem((2, width // span, rows, span), bf16),
    ]
    if shared:
        scratch += [vmem(part.shape, bf16) for part in shared]
        scratch += [vmem((2 * rows, shared_hidden), bf16)]
    scratch += [
        sems((2 * count,)),
        sems((hidden // tile,)),
        sems((hidden // tile,)),
        sems((width // span,)),
        sems((2, width // span)),
    ]
    if shared:
        scratch += [sems((3,))]
    token = np.arange(rows)
    before = (token[:, None] < token) & (token[:, None] // block == token // block)
    base = np.broadcast_to(token // block * most, (16, rows))
    before = jnp.asarray(np.concatenate([before, base], axis=0), bf16)
    operands = [*mine, *other, before, *weights, *(shared or ()), *after]
    flops = 2 * (6 * slots * width * hidden + 4 * rows * slots * width)
    flops += 2 * 6 * rows * width * shared_hidden
    moved = 2 * (sum(part.size for part in operands[: len(operands) - len(after)]) + 2 * rows * width)
    return pl.pallas_call(
        functools.partial(expert_body, dims, len(scratch) + 2),
        out_shape=[jax.ShapeDtypeStruct((rows, width), bf16)] * 2,
        in_specs=[
            pl.BlockSpec(memory_space=pltpu.VMEM if part is before else pl.ANY) for part in operands
        ],
        out_specs=[pl.BlockSpec(memory_space=pl.ANY)] * 2,
        scratch_shapes=scratch,
        compiler_params=pltpu.CompilerParams(vmem_limit_bytes=52 * 1024 * 1024),
        cost_estimate=pl.CostEstimate(flops=flops, bytes_accessed=moved, transcendentals=0),
    )(*operands)


def gather_all(
    tokens, route_ids, route_weight, w_gate, w_up, w_down, shared_gate, shared_up, shared_down
):
    block = tokens.shape[0]
    planes = lax.axis_size("ey")
    experts = lax.axis_size("ex") * planes
    most = max(2, 2 * block * route_ids.shape[1] // experts)
    hit = route_ids[:, :, None] == jnp.arange(LANES, dtype=jnp.int32)
    table = jnp.sum(jnp.where(hit, route_weight[:, :, None], 0).astype(jnp.float32), axis=1)
    own = jnp.concatenate([tokens, table.astype(tokens.dtype)], axis=1)
    columns = [own] + [swap(own, "ey", mask) for mask in range(1, planes)]
    order = [0] + list(range(2, planes)) + [1]
    last = len(order) - 1
    pieces = [gather_plane(columns[mask], turn % 2) for turn, mask in enumerate(order)]
    mine, got, across, plain, full, parts = {}, {}, {}, {}, {}, {}

    def job_across(k):
        return [(mine[k], 3), (got[k], 3)]

    def job_plain(k):
        piece = 1 if k % 2 else 2
        return [(mine[k], piece), (got[k], piece)]

    def job_full(k):
        piece = 2 if k % 2 else 1
        return [(mine[k], piece), (got[k], piece), (across[k], 0)]

    def job_part(k):
        return [(mine[k], 0), (got[k], 0), (plain[k], 0), (full[k], 0)]

    after = ()
    for k in range(len(order) + 2):
        jobs, sends = [], []
        if k <= last:
            own_pieces = pieces[k]
            other = [swap(piece, "ex", PAIR) for piece in own_pieces]
            shared = (shared_gate, shared_up, shared_down) if order[k] == 0 else None
            mine[k], theirs = run_expert(
                own_pieces, other, most, (w_gate, w_up, w_down), shared, after
            )
            got[k] = swap(theirs, "ex", PAIR)
            jobs += [job_across(k), job_plain(k)]
            sends += [
                (across, k, "ex", RIGHT if k % 2 else DOWN),
                (plain, k, "ex", RIGHT if k % 2 else DOWN),
            ]
        if 0 <= k - 1 <= last:
            jobs.append(job_full(k - 1))
            sends.append((full, k - 1, "ex", DOWN if (k - 1) % 2 else RIGHT))
        if 0 < k - 2 <= last:
            jobs.append(job_part(k - 2))
            sends.append((parts, k - 2, "ey", order[k - 2]))
        summed = add_rows(block, jobs)
        after = (summed[0],)
        for value, (store, phase, axis, mask) in zip(summed, sends):
            store[phase] = swap(value, axis, mask)
    jobs = [job_part(0) + [(parts[k], 0) for k in range(1, len(order))]]
    return add_rows(block, jobs)[0]


def solution(mesh):
    sizes = dict(mesh.shape)

    def shards(*args):
        tokens, route_ids = args[0], args[1]
        slots = max(2, 2 * tokens.shape[0] * route_ids.shape[1] // (sizes["ex"] * sizes["ey"]))
        cube = sizes["ex"] == 2 * DOWN and sizes["ey"] & (sizes["ey"] - 1) == 0
        cube = cube and sizes["ex"] * sizes["ey"] <= LANES
        if cube and 4 * slots > tokens.shape[0]:
            return gather_all(*args)
        return exchange_slots(*args)

    in_specs = (
        P(("ex", "ey"), None),
        P(("ex", "ey"), None),
        P(("ex", "ey"), None),
        P(("ex", "ey"), None, None),
        P(("ex", "ey"), None, None),
        P(("ex", "ey"), None, None),
        P(None, "ex"),
        P(None, "ex"),
        P("ex", None),
    )
    out_specs = P(("ex", "ey"), None)
    return jax.shard_map(shards, mesh=mesh, in_specs=in_specs, out_specs=out_specs, check_vma=False)
```

```python
import functools

import jax
import jax.numpy as jnp
import numpy as np
from jax import lax
from jax.experimental import pallas as pl
from jax.experimental.pallas import tpu as pltpu
from jax.sharding import PartitionSpec as P


def swiglu(chosen, gate_weight, up_weight, down_weight):
    gate_act = jnp.dot(chosen, gate_weight, preferred_element_type=jnp.float32)
    up_act = jnp.dot(chosen, up_weight, preferred_element_type=jnp.float32)
    hidden = (jax.nn.silu(gate_act) * up_act).astype(jnp.bfloat16)
    return jnp.dot(hidden, down_weight, preferred_element_type=jnp.float32)


def shared_expert(tokens, shared_gate, shared_up, shared_down):
    gathered = lax.all_gather(tokens, "ex", axis=0, tiled=True)
    return lax.psum_scatter(
        swiglu(gathered, shared_gate, shared_up, shared_down).astype(jnp.bfloat16),
        "ex",
        scatter_dimension=0,
        tiled=True,
    ).astype(jnp.float32)


def exchange_slots(
    tokens, route_ids, route_weight, w_gate, w_up, w_down, shared_gate, shared_up, shared_down
):
    tok_rows = tokens.shape[0]
    top_count = route_ids.shape[1]
    width = tokens.shape[1]
    experts = lax.axis_size("ex") * lax.axis_size("ey")
    slot_most = max(2, 2 * tok_rows * top_count // experts)
    capacity = experts * slot_most
    flat_ids = route_ids.reshape(-1)
    onehot = (flat_ids[:, None] == jnp.arange(experts, dtype=jnp.int32)[None, :]).astype(jnp.int32)
    slot_rank = jnp.sum((jnp.cumsum(onehot, axis=0) - onehot) * onehot, axis=1)
    slot_place = flat_ids * slot_most + slot_rank
    matches = (slot_place[:, None] == jnp.arange(capacity, dtype=jnp.int32)[None, :]).astype(
        jnp.float32
    )
    matches = matches.reshape(tok_rows, top_count, capacity)
    placing = jnp.sum(matches, axis=1).astype(jnp.bfloat16)
    combine_mat = jnp.sum(matches * route_weight.astype(jnp.float32)[:, :, None], axis=1).astype(
        jnp.bfloat16
    )
    outgoing = jnp.einsum("tc,td->cd", placing, tokens, preferred_element_type=jnp.float32).astype(
        jnp.bfloat16
    )
    outgoing = outgoing.reshape(experts, slot_most, width)
    arrived = lax.all_to_all(outgoing, ("ex", "ey"), split_axis=0, concat_axis=0, tiled=True)
    layout = arrived.shape
    result = swiglu(arrived.reshape(-1, width), w_gate[0], w_up[0], w_down[0])
    produced = result.astype(jnp.bfloat16).reshape(layout)
    returned = lax.all_to_all(produced, ("ex", "ey"), split_axis=0, concat_axis=0, tiled=True)
    returned = returned.reshape(capacity, width)
    routed = jnp.dot(combine_mat, returned, preferred_element_type=jnp.float32)
    shared = shared_expert(tokens, shared_gate, shared_up, shared_down)
    return (shared + routed).astype(jnp.bfloat16)


PAIR, RIGHT, DOWN = 1, 2, 4


def swap(value, axis, mask):
    size = lax.axis_size(axis)
    return lax.ppermute(value, axis, [(i, i ^ mask) for i in range(size)])


def add_body(jobs, *refs):
    outs = refs[len(refs) - len(jobs) :]
    at = 0
    for out, job in zip(outs, jobs):
        total = refs[at][...].astype(jnp.float32)
        for k in range(1, job):
            total += refs[at + k][...].astype(jnp.float32)
        out[...] = total.astype(out.dtype)
        at += job


def in_hbm(array):
    return pltpu.with_memory_space_constraint(array, pltpu.HBM)


def add_rows(rows, jobs):
    width = jobs[0][0][0].shape[1]
    steps = 2
    span = width // steps

    def spec(block):
        return pl.BlockSpec((rows, span), lambda j: (block, j))

    return pl.pallas_call(
        functools.partial(add_body, tuple(len(job) for job in jobs)),
        grid=(steps,),
        out_shape=[pltpu.HBM((rows, width), jnp.bfloat16)] * len(jobs),
        in_specs=[spec(block) for job in jobs for _, block in job],
        out_specs=[spec(0)] * len(jobs),
        cost_estimate=pl.CostEstimate(
            flops=sum(map(len, jobs)) * rows * width,
            bytes_accessed=2 * (sum(map(len, jobs)) + len(jobs)) * rows * width,
            transcendentals=0,
        ),
    )(*[in_hbm(array) for job in jobs for array, _ in job])


LANES = 128


def tile_of(size, goal):
    return max(t for t in range(LANES, goal + 1, LANES) if size % t == 0)


def expert_body(dims, *refs):
    sides, block, most, width, hidden, shared_hidden, tile, span, ring = dims
    pieces_of = 4
    rows = pieces_of * block
    slots = pieces_of * most
    refs = list(refs)

    def take(number):
        out = refs[:number]
        del refs[:number]
        return out

    pieces = take(sides * pieces_of)
    (before_ref,) = take(1)
    experts = [take(3), take(3)]
    shared = [take(3), take(3)] if shared_hidden else []
    take(len(refs) - 15 - sides * pieces_of)
    outs = take(sides * pieces_of)
    held, chosen, gate, up, down, down_s, act, act_s, back, result = take(10)
    piece_sem, step_sem, span_sem, span_s_sem, out_sem = take(5)
    copy = pltpu.make_async_copy
    f32, bf16 = jnp.float32, jnp.bfloat16

    steps = [(part[0], part[1], None) for part in shared]
    steps += [
        (part[0].at[0], part[1].at[0], k * tile) for part in experts for k in range(hidden // tile)
    ]
    spans = width // span

    def piece_copy(k):
        return copy(pieces[k], held.at[pl.ds(k * block, block), :], piece_sem.at[k])

    def step_copies(k):
        at = k % ring
        low = steps[k][2] or 0
        return [
            copy(steps[k][0].at[:, pl.ds(low, tile)], gate.at[at], step_sem.at[0, at]),
            copy(steps[k][1].at[:, pl.ds(low, tile)], up.at[at], step_sem.at[1, at]),
        ]

    def span_copies(k):
        at = k % ring
        columns = pl.ds(k * span, span)
        both = [
            copy(part[2].at[0, :, columns], down.at[at, e], span_sem.at[at, e])
            for e, part in enumerate(experts)
        ]
        return both + [
            copy(part[2].at[:, columns], down_s.at[at, e], span_s_sem.at[at, e])
            for e, part in enumerate(shared)
        ]

    def out_copy(side, piece, k):
        return copy(
            result.at[side, k, pl.ds(piece * block, block), :],
            outs[side * pieces_of + piece].at[:, pl.ds(k * span, span)],
            out_sem.at[side, piece, k],
        )

    def start(copies):
        for one in copies:
            one.start()

    def wait(copies):
        for one in copies:
            one.wait()

    start([piece_copy(k) for k in range(sides * pieces_of)])
    start(step_copies(0))

    ey = lax.axis_size("ey")
    ex = lax.axis_index("ex")
    me = ex * ey + lax.axis_index("ey")
    partner = (ex + PAIR - 2 * PAIR * (ex % (2 * PAIR))) * ey + lax.axis_index("ey")
    row = lax.broadcasted_iota(jnp.int32, (16, LANES), 0)
    lane = lax.broadcasted_iota(jnp.int32, (16, LANES), 1)
    pick = (lane == jnp.where(row == 0, me, partner)).astype(f32).astype(bf16)
    before = before_ref[:rows]
    base = before_ref[rows : rows + 16].astype(f32)[0:1]
    slot = lax.broadcasted_iota(jnp.int32, (slots, rows), 0).astype(f32)
    for side in range(sides):
        wait([piece_copy(k) for k in range(side * pieces_of, (side + 1) * pieces_of)])
        if side == 0:
            for k in range(1, ring):
                start(step_copies(k))
        low = side * rows
        table = held[low : low + rows, width : width + LANES]
        rate = lax.dot_general(
            pick, table, (((1,), (1,)), ((), ())), preferred_element_type=f32
        )
        named = (rate > 0).astype(f32)
        rank = jnp.dot(named.astype(bf16), before, preferred_element_type=f32)
        places = []
        for e in range(2):
            where = jnp.where(named[e : e + 1] > 0, rank[e : e + 1] + base, -1.0)
            place = slot == where
            back[side, :, e * slots : (e + 1) * slots] = jnp.where(
                place, rate[e : e + 1], 0.0
            ).T.astype(bf16)
            places.append(place.astype(f32).astype(bf16))
        picked = jnp.dot(
            jnp.concatenate(places, axis=0),
            held[low : low + rows, :width],
            preferred_element_type=f32,
        ).astype(bf16)
        for e in range(2):
            chosen[e, side * slots : (side + 1) * slots] = picked[e * slots : (e + 1) * slots]

    per = hidden // tile
    for k in range(len(steps)):
        wait(step_copies(k))
        e, at = divmod(k - len(shared), per)
        source = held[:rows, :width] if k < len(shared) else chosen[e]
        g = jnp.dot(source, gate[k % ring], preferred_element_type=f32)
        u = jnp.dot(source, up[k % ring], preferred_element_type=f32)
        h = (jax.nn.silu(g) * u).astype(bf16)
        if k < len(shared):
            act_s[k] = h
        else:
            act[e, :, at * tile : (at + 1) * tile] = h
        if k + ring < len(steps):
            start(step_copies(k + ring))
        elif k + ring - len(steps) < min(ring, spans):
            start(span_copies(k + ring - len(steps)))

    for k in range(spans):
        wait(span_copies(k))
        y = [
            jnp.dot(act[e], down[k % ring, e], preferred_element_type=f32).astype(bf16)
            for e in range(2)
        ]
        for side in range(sides):
            mine = [part[side * slots : (side + 1) * slots] for part in y]
            out = jnp.dot(back[side], jnp.concatenate(mine, axis=0), preferred_element_type=f32)
            if side == 0:
                for e in range(len(shared)):
                    out += jnp.dot(act_s[e], down_s[k % ring, e], preferred_element_type=f32)
            result[side, k] = out.astype(bf16)
            start([out_copy(side, piece, k) for piece in range(pieces_of)])
        if k + ring < spans:
            start(span_copies(k + ring))

    wait(
        [
            out_copy(side, piece, k)
            for side in range(sides)
            for piece in range(pieces_of)
            for k in range(spans)
        ]
    )


def run_experts(sides, most, experts, shared, after=()):
    block, wide = sides[0][0].shape
    width, hidden = wide - LANES, experts[0][0].shape[2]
    shared_hidden = shared[0][0].shape[1] if shared else 0
    tile, span, ring = shared_hidden or tile_of(hidden, 256), tile_of(width, 512), 3
    number, pieces_of = len(sides), len(sides[0])
    rows, slots = pieces_of * block, pieces_of * most
    dims = (number, block, most, width, hidden, shared_hidden, tile, span, ring)
    bf16 = jnp.bfloat16
    vmem, sems = pltpu.VMEM, pltpu.SemaphoreType.DMA
    shared_rows = shared_hidden or 16
    scratch = [
        vmem((number * rows, wide), bf16),
        vmem((2, number * slots, width), bf16),
        vmem((ring, width, tile), bf16),
        vmem((ring, width, tile), bf16),
        vmem((ring, 2, hidden, span), bf16),
        vmem((ring, 2, shared_rows, span), bf16),
        vmem((2, number * slots, hidden), bf16),
        vmem((2, rows, max(shared_rows, LANES)), bf16),
        vmem((number, rows, 2 * slots), bf16),
        vmem((number, width // span, rows, span), bf16),
        sems((number * pieces_of,)),
        sems((2, ring)),
        sems((ring, 2)),
        sems((ring, 2)),
        sems((number, pieces_of, width // span)),
    ]
    token = np.arange(rows)
    before = (token[:, None] < token) & (token[:, None] // block == token // block)
    base = np.broadcast_to(token // block * most, (16, rows))
    before = jnp.asarray(np.concatenate([before, base], axis=0), bf16)
    operands = [part for side in sides for part in side] + [before]
    operands += [part for weights in (*experts, *shared) for part in weights]
    moved = 2 * (sum(part.size for part in operands) + number * rows * width)
    flops = 2 * number * (6 * slots * width * hidden + 4 * rows * slots * width)
    flops += 12 * rows * width * shared_hidden
    operands += after
    operands = [part if part is before else in_hbm(part) for part in operands]
    return pl.pallas_call(
        functools.partial(expert_body, dims),
        out_shape=[pltpu.HBM((block, width), bf16)] * (number * pieces_of),
        in_specs=[
            pl.BlockSpec(memory_space=pltpu.VMEM if part is before else pl.ANY) for part in operands
        ],
        out_specs=[pl.BlockSpec(memory_space=pl.ANY)] * (number * pieces_of),
        scratch_shapes=scratch,
        compiler_params=pltpu.CompilerParams(vmem_limit_bytes=50 * 1024 * 1024),
        cost_estimate=pl.CostEstimate(flops=flops, bytes_accessed=moved, transcendentals=0),
    )(*operands)


def pin(done, moving):
    count = len(done)
    both = lax.optimization_barrier((*done, *moving))
    return list(both[:count]), list(both[count:])


def gather_all(
    tokens, route_ids, route_weight, w_gate, w_up, w_down, shared_gate, shared_up, shared_down
):
    block = tokens.shape[0]
    experts = lax.axis_size("ex") * lax.axis_size("ey")
    most = max(2, 2 * block * route_ids.shape[1] // experts)
    hit = route_ids[:, :, None] == jnp.arange(LANES, dtype=jnp.int32)
    table = jnp.sum(jnp.where(hit, route_weight[:, :, None], 0).astype(jnp.float32), axis=1)
    own = jnp.concatenate([tokens, table.astype(tokens.dtype)], axis=1)
    def right(value):
        return swap(value, "ex", RIGHT)

    def down(value):
        return swap(value, "ex", DOWN)

    def pair(value):
        return swap(value, "ex", PAIR)

    def far(value, mask):
        return swap(value, "ey", mask)

    tie = lax.optimization_barrier
    z2, r0, d0, w_gate_o, w_up_o = far(own, 2), right(own), down(own), pair(w_gate), pair(w_up)
    z2, r0, d0, w_gate_o, w_up_o, w_down_t, shared_down_t = tie(
        (z2, r0, d0, w_gate_o, w_up_o, w_down, shared_down)
    )
    r2, d2, z3, w_down_o, shared_down_o = (
        right(z2), down(z2), far(z2, 1), pair(w_down_t), pair(shared_down_t)
    )
    r0, r2, d2, z3, w_down_o, shared_down_o, shared_gate_t, shared_up_t, own_t = tie(
        (r0, r2, d2, z3, w_down_o, shared_down_o, shared_gate, shared_up, own)
    )
    a2, a0, z1, shared_gate_o, shared_up_o = (
        right(d2), down(r0), far(own_t, 1), pair(shared_gate_t), pair(shared_up_t)
    )
    a2, a0, z1, shared_gate_o, shared_up_o, z3 = tie(
        (a2, a0, z1, shared_gate_o, shared_up_o, z3)
    )
    experts = [(w_gate, w_up, w_down), (w_gate_o, w_up_o, w_down_o)]
    shared = [
        (shared_gate, shared_up, shared_down),
        (shared_gate_o, shared_up_o, shared_down_o),
    ]
    r3, d3, r1, d1 = right(z3), down(z3), right(z1), down(z1)
    out = run_experts([[own, r0, d0, a0], [z2, r2, d2, a2]], most, experts, shared)
    out, (r3, d3, r1, d1) = pin(out, (r3, d3, r1, d1))
    sum0, sum2 = out[:4], out[4:]
    a3, a1 = down(r3), right(d1)
    across0, across2 = down(sum0[3]), right(sum2[3])
    (a3, a1), (across0, across2) = pin((a3, a1), (across0, across2))
    full0, full2 = add_rows(
        block, [[(sum0[1], 0), (across0, 0)], [(sum2[2], 0), (across2, 0)]]
    )
    sent0, sent2 = right(full0), down(full2)
    plain0, plain2 = down(sum0[2]), right(sum2[1])
    out = run_experts([[z3, r3, d3, a3], [z1, r1, d1, a1]], most, experts, [], (full0,))
    out, (full0, full2, plain0, plain2) = pin(out, (sent0, sent2, plain0, plain2))
    sum3, sum1 = out[:4], out[4:]
    across3, across1 = down(sum3[3]), right(sum1[3])
    part2 = add_rows(block, [[(sum2[0], 0), (plain2, 0), (full2, 0)]])
    (part2,), (across3, across1) = pin(part2, (across3, across1))
    back2 = far(part2, 2)
    full3, full1 = add_rows(
        block, [[(sum3[1], 0), (across3, 0)], [(sum1[2], 0), (across1, 0)]]
    )
    full3, plain3 = right(full3), down(sum3[2])
    (part3,) = add_rows(block, [[(sum3[0], 0), (plain3, 0), (full3, 0)]])
    full1, plain1, part3 = lax.optimization_barrier((full1, sum1[1], part3))
    full1, plain1, back3 = down(full1), right(plain1), far(part3, 3)
    part1 = add_rows(block, [[(sum1[0], 0), (plain1, 0), (full1, 0)]])
    part1, (back2,) = pin(part1, (back2,))
    back1 = far(part1[0], 1)
    total = [(sum0[0], 0), (plain0, 0), (full0, 0), (back2, 0), (back3, 0), (back1, 0)]
    return add_rows(block, [total])[0]


def solution(mesh):
    sizes = dict(mesh.shape)

    def shards(*args):
        tokens, route_ids = args[0], args[1]
        slots = max(2, 2 * tokens.shape[0] * route_ids.shape[1] // (sizes["ex"] * sizes["ey"]))
        cube = sizes["ex"] == 2 * DOWN and sizes["ey"] == 4
        if cube and 4 * slots > tokens.shape[0]:
            return gather_all(*args)
        return exchange_slots(*args)

    in_specs = (
        P(("ex", "ey"), None),
        P(("ex", "ey"), None),
        P(("ex", "ey"), None),
        P(("ex", "ey"), None, None),
        P(("ex", "ey"), None, None),
        P(("ex", "ey"), None, None),
        P(None, "ex"),
        P(None, "ex"),
        P("ex", None),
    )
    out_specs = P(("ex", "ey"), None)
    return jax.shard_map(shards, mesh=mesh, in_specs=in_specs, out_specs=out_specs, check_vma=False)
```

```python
import functools

import jax
import jax.numpy as jnp
import numpy as np
from jax import lax
from jax.experimental import pallas as pl
from jax.experimental.pallas import tpu as pltpu
from jax.sharding import PartitionSpec as P


def swiglu(chosen, gate_weight, up_weight, down_weight):
    gate_act = jnp.dot(chosen, gate_weight, preferred_element_type=jnp.float32)
    up_act = jnp.dot(chosen, up_weight, preferred_element_type=jnp.float32)
    hidden = (jax.nn.silu(gate_act) * up_act).astype(jnp.bfloat16)
    return jnp.dot(hidden, down_weight, preferred_element_type=jnp.float32)


def shared_expert(tokens, shared_gate, shared_up, shared_down):
    gathered = lax.all_gather(tokens, "ex", axis=0, tiled=True)
    return lax.psum_scatter(
        swiglu(gathered, shared_gate, shared_up, shared_down).astype(jnp.bfloat16),
        "ex",
        scatter_dimension=0,
        tiled=True,
    ).astype(jnp.float32)


def exchange_slots(
    tokens, route_ids, route_weight, w_gate, w_up, w_down, shared_gate, shared_up, shared_down
):
    tok_rows = tokens.shape[0]
    top_count = route_ids.shape[1]
    width = tokens.shape[1]
    experts = lax.axis_size("ex") * lax.axis_size("ey")
    slot_most = max(2, 2 * tok_rows * top_count // experts)
    capacity = experts * slot_most
    flat_ids = route_ids.reshape(-1)
    onehot = (flat_ids[:, None] == jnp.arange(experts, dtype=jnp.int32)[None, :]).astype(jnp.int32)
    slot_rank = jnp.sum((jnp.cumsum(onehot, axis=0) - onehot) * onehot, axis=1)
    slot_place = flat_ids * slot_most + slot_rank
    matches = (slot_place[:, None] == jnp.arange(capacity, dtype=jnp.int32)[None, :]).astype(
        jnp.float32
    )
    matches = matches.reshape(tok_rows, top_count, capacity)
    placing = jnp.sum(matches, axis=1).astype(jnp.bfloat16)
    combine_mat = jnp.sum(matches * route_weight.astype(jnp.float32)[:, :, None], axis=1).astype(
        jnp.bfloat16
    )
    outgoing = jnp.einsum("tc,td->cd", placing, tokens, preferred_element_type=jnp.float32).astype(
        jnp.bfloat16
    )
    outgoing = outgoing.reshape(experts, slot_most, width)
    arrived = lax.all_to_all(outgoing, ("ex", "ey"), split_axis=0, concat_axis=0, tiled=True)
    layout = arrived.shape
    result = swiglu(arrived.reshape(-1, width), w_gate[0], w_up[0], w_down[0])
    produced = result.astype(jnp.bfloat16).reshape(layout)
    returned = lax.all_to_all(produced, ("ex", "ey"), split_axis=0, concat_axis=0, tiled=True)
    returned = returned.reshape(capacity, width)
    routed = jnp.dot(combine_mat, returned, preferred_element_type=jnp.float32)
    shared = shared_expert(tokens, shared_gate, shared_up, shared_down)
    return (shared + routed).astype(jnp.bfloat16)


PAIR, RIGHT, DOWN = 1, 2, 4
VMEM_LIMIT = 60 * 1024 * 1024
VMEM_ALL = 64 * 1024 * 1024 - 256 * 1024


def swap(value, axis, mask):
    size = lax.axis_size(axis)
    return lax.ppermute(value, axis, [(i, i ^ mask) for i in range(size)])


def add_body(jobs, *refs):
    outs = refs[len(refs) - len(jobs) :]
    at = 0
    for out, job in zip(outs, jobs):
        total = refs[at][...].astype(jnp.float32)
        for k in range(1, job):
            total += refs[at + k][...].astype(jnp.float32)
        out[...] = total.astype(out.dtype)
        at += job


def in_hbm(array):
    return pltpu.with_memory_space_constraint(array, pltpu.HBM)


def add_rows(rows, jobs, dtype=jnp.bfloat16):
    width = jobs[0][0][0].shape[1]
    steps = 2
    span = width // steps

    def spec(block):
        return pl.BlockSpec((rows, span), lambda j: (block, j))

    return pl.pallas_call(
        functools.partial(add_body, tuple(len(job) for job in jobs)),
        grid=(steps,),
        out_shape=[pltpu.HBM((rows, width), dtype)] * len(jobs),
        in_specs=[spec(block) for job in jobs for _, block in job],
        out_specs=[spec(0)] * len(jobs),
        compiler_params=pltpu.CompilerParams(vmem_limit_bytes=VMEM_ALL),
        cost_estimate=pl.CostEstimate(
            flops=sum(map(len, jobs)) * rows * width,
            bytes_accessed=2 * (sum(map(len, jobs)) + len(jobs)) * rows * width,
            transcendentals=0,
        ),
    )(*[in_hbm(array) for job in jobs for array, _ in job])


LANES = 128


def tile_of(size, goal):
    return max(t for t in range(LANES, goal + 1, LANES) if size % t == 0)


def table_body(tokens, ids, rates, out):
    top, rows = ids.shape
    width = tokens.shape[1]
    expert = lax.broadcasted_iota(jnp.int32, (LANES, rows), 0)
    table = jnp.zeros((LANES, rows), jnp.float32)
    for k in range(top):
        hit = ids[k : k + 1, :] == expert
        table += jnp.where(hit, rates[k : k + 1, :].astype(jnp.float32), 0.0)
    out[:, :width] = tokens[...]
    out[:, width:] = table.T.astype(out.dtype)


def with_table(tokens, ids, rates):
    rows, width = tokens.shape
    return pl.pallas_call(
        table_body,
        out_shape=jax.ShapeDtypeStruct((rows, width + LANES), tokens.dtype),
    )(tokens, ids.T, rates.T)


def expert_body(dims, *refs):
    sides, block, most, width, hidden, shared_hidden, tile, span, ring = dims
    pieces_of = 4
    rows = pieces_of * block
    slots = pieces_of * most
    refs = list(refs)

    def take(number):
        out = refs[:number]
        del refs[:number]
        return out

    pieces = take(sides * pieces_of)
    (before_ref,) = take(1)
    experts = [take(3), take(3)]
    shared = [take(3), take(3)] if shared_hidden else []
    take(len(refs) - 15 - sides * pieces_of)
    outs = take(sides * pieces_of)
    held, chosen, gate, up, down, down_s, act, act_s, back, result = take(10)
    piece_sem, step_sem, span_sem, span_s_sem, out_sem = take(5)
    copy = pltpu.make_async_copy
    f32, bf16 = jnp.float32, jnp.bfloat16

    steps = [(part[0], part[1], low) for part, low in zip(shared, (0, shared_hidden))]
    steps += [
        (part[0].at[0], part[1].at[0], k * tile) for part in experts for k in range(hidden // tile)
    ]
    spans = width // span

    def piece_copy(k):
        return copy(pieces[k], held.at[pl.ds(k * block, block), :], piece_sem.at[k])

    def step_copies(k):
        at = k % ring
        low = steps[k][2]
        gate_low = 0 if k < len(shared) else low
        return [
            copy(steps[k][0].at[:, pl.ds(gate_low, tile)], gate.at[at], step_sem.at[0, at]),
            copy(steps[k][1].at[:, pl.ds(low, tile)], up.at[at], step_sem.at[1, at]),
        ]

    def span_copies(k):
        at = k % ring
        columns = pl.ds(k * span, span)
        both = [
            copy(part[2].at[0, :, columns], down.at[at, e], span_sem.at[at, e])
            for e, part in enumerate(experts)
        ]
        return both + [
            copy(part[2].at[:, columns], down_s.at[at, e], span_s_sem.at[at, e])
            for e, part in enumerate(shared)
        ]

    def out_copy(side, piece, k):
        return copy(
            result.at[side, k, pl.ds(piece * block, block), :],
            outs[side * pieces_of + piece].at[:, pl.ds(k * span, span)],
            out_sem.at[side, piece, k],
        )

    def start(copies):
        for one in copies:
            one.start()

    def wait(copies):
        for one in copies:
            one.wait()

    start([piece_copy(k) for k in range(sides * pieces_of)])
    start(step_copies(0))

    ey = lax.axis_size("ey")
    ex = lax.axis_index("ex")
    me = ex * ey + lax.axis_index("ey")
    partner = (ex + PAIR - 2 * PAIR * (ex % (2 * PAIR))) * ey + lax.axis_index("ey")
    row = lax.broadcasted_iota(jnp.int32, (16, LANES), 0)
    lane = lax.broadcasted_iota(jnp.int32, (16, LANES), 1)
    pick = (lane == jnp.where(row == 0, me, partner)).astype(f32).astype(bf16)
    before = before_ref[:rows]
    base = before_ref[rows : rows + 16].astype(f32)[0:1]
    slot = lax.broadcasted_iota(jnp.int32, (slots, rows), 0).astype(f32)
    for side in range(sides):
        wait([piece_copy(k) for k in range(side * pieces_of, (side + 1) * pieces_of)])
        if side == 0:
            for k in range(1, ring):
                start(step_copies(k))
        low = side * rows
        table = held[low : low + rows, width : width + LANES]
        rate = lax.dot_general(
            pick, table, (((1,), (1,)), ((), ())), preferred_element_type=f32
        )
        named = (rate > 0).astype(f32)
        rank = jnp.dot(named.astype(bf16), before, preferred_element_type=f32)
        places = []
        for e in range(2):
            where = jnp.where(named[e : e + 1] > 0, rank[e : e + 1] + base, -1.0)
            place = slot == where
            back[side, :, e * slots : (e + 1) * slots] = jnp.where(
                place, rate[e : e + 1], 0.0
            ).T.astype(bf16)
            places.append(place.astype(f32).astype(bf16))
        picked = jnp.dot(
            jnp.concatenate(places, axis=0),
            held[low : low + rows, :width],
            preferred_element_type=f32,
        ).astype(bf16)
        for e in range(2):
            chosen[e, side * slots : (side + 1) * slots] = picked[e * slots : (e + 1) * slots]

    per = hidden // tile
    for k in range(len(steps)):
        wait(step_copies(k))
        e, at = divmod(k - len(shared), per)
        source = held[:rows, :width] if k < len(shared) else chosen[e]
        g = jnp.dot(source, gate[k % ring], preferred_element_type=f32)
        u = jnp.dot(source, up[k % ring], preferred_element_type=f32)
        h = (jax.nn.silu(g) * u).astype(bf16)
        if k < len(shared):
            act_s[k] = h
        else:
            act[e, :, at * tile : (at + 1) * tile] = h
        if k + ring < len(steps):
            start(step_copies(k + ring))
        elif k + ring - len(steps) < min(ring, spans):
            start(span_copies(k + ring - len(steps)))

    for k in range(spans):
        wait(span_copies(k))
        y = [
            jnp.dot(act[e], down[k % ring, e], preferred_element_type=f32).astype(bf16)
            for e in range(2)
        ]
        for side in range(sides):
            mine = [part[side * slots : (side + 1) * slots] for part in y]
            out = jnp.dot(back[side], jnp.concatenate(mine, axis=0), preferred_element_type=f32)
            if side == 0:
                for e in range(len(shared)):
                    out += jnp.dot(act_s[e], down_s[k % ring, e], preferred_element_type=f32)
            result[side, k] = out.astype(bf16)
            start([out_copy(side, piece, k) for piece in range(pieces_of)])
        if k + ring < spans:
            start(span_copies(k + ring))

    wait(
        [
            out_copy(side, piece, k)
            for side in range(sides)
            for piece in range(pieces_of)
            for k in range(spans)
        ]
    )


def run_experts(sides, most, experts, shared, after=()):
    block, wide = sides[0][0].shape
    width, hidden = wide - LANES, experts[0][0].shape[2]
    shared_hidden = shared[0][0].shape[1] if shared else 0
    tile, span, ring = shared_hidden or tile_of(hidden, 256), tile_of(width, 512), 3
    number, pieces_of = len(sides), len(sides[0])
    rows, slots = pieces_of * block, pieces_of * most
    dims = (number, block, most, width, hidden, shared_hidden, tile, span, ring)
    bf16 = jnp.bfloat16
    vmem, sems = pltpu.VMEM, pltpu.SemaphoreType.DMA
    shared_rows = shared_hidden or 16
    scratch = [
        vmem((number * rows, wide), bf16),
        vmem((2, number * slots, width), bf16),
        vmem((ring, width, tile), bf16),
        vmem((ring, width, tile), bf16),
        vmem((ring, 2, hidden, span), bf16),
        vmem((ring, 2, shared_rows, span), bf16),
        vmem((2, number * slots, hidden), bf16),
        vmem((2, rows, max(shared_rows, LANES)), bf16),
        vmem((number, rows, 2 * slots), bf16),
        vmem((number, width // span, rows, span), bf16),
        sems((number * pieces_of,)),
        sems((2, ring)),
        sems((ring, 2)),
        sems((ring, 2)),
        sems((number, pieces_of, width // span)),
    ]
    token = np.arange(rows)
    before = (token[:, None] < token) & (token[:, None] // block == token // block)
    base = np.broadcast_to(token // block * most, (16, rows))
    before = jnp.asarray(np.concatenate([before, base], axis=0), bf16)
    operands = [part for side in sides for part in side] + [before]
    operands += [part for weights in (*experts, *shared) for part in weights]
    moved = 2 * (sum(part.size for part in operands) + number * rows * width)
    flops = 2 * number * (6 * slots * width * hidden + 4 * rows * slots * width)
    flops += 12 * rows * width * shared_hidden
    operands += after
    operands = [part if part is before else in_hbm(part) for part in operands]
    return pl.pallas_call(
        functools.partial(expert_body, dims),
        out_shape=[pltpu.HBM((block, width), bf16)] * (number * pieces_of),
        in_specs=[
            pl.BlockSpec(memory_space=pltpu.VMEM if part is before else pl.ANY) for part in operands
        ],
        out_specs=[pl.BlockSpec(memory_space=pl.ANY)] * (number * pieces_of),
        scratch_shapes=scratch,
        compiler_params=pltpu.CompilerParams(vmem_limit_bytes=VMEM_LIMIT),
        cost_estimate=pl.CostEstimate(flops=flops, bytes_accessed=moved, transcendentals=0),
    )(*operands)


def pin(done, moving):
    count = len(done)
    both = lax.optimization_barrier((*done, *moving))
    return list(both[:count]), list(both[count:])


def gather_all(
    tokens, route_ids, route_weight, w_gate, w_up, w_down, shared_gate, shared_up, shared_down
):
    block = tokens.shape[0]
    experts = lax.axis_size("ex") * lax.axis_size("ey")
    most = max(2, 2 * block * route_ids.shape[1] // experts)
    own = with_table(tokens, route_ids, route_weight)
    def right(value):
        return swap(value, "ex", RIGHT)

    def down(value):
        return swap(value, "ex", DOWN)

    def pair(value):
        return swap(value, "ex", PAIR)

    def far(value, mask):
        return swap(value, "ey", mask)

    tie = lax.optimization_barrier
    z2, r0, d0, w_gate_o, w_up_o = far(own, 2), right(own), down(own), pair(w_gate), pair(w_up)
    packed = jnp.concatenate([shared_gate, shared_up], axis=1)
    z2, r0, d0, w_gate_o, w_up_o, w_down_t, packed = tie(
        (z2, r0, d0, w_gate_o, w_up_o, w_down, packed)
    )
    r2, d2, z3, w_down_o = right(z2), down(z2), far(z2, 1), pair(w_down_t)
    r0, r2, d2, z3, w_down_o, packed, shared_down_t, own_t = tie(
        (r0, r2, d2, z3, w_down_o, packed, shared_down, own)
    )
    a2, a0, z1, packed_o, shared_down_o = (
        right(d2), down(r0), far(own_t, 1), pair(packed), pair(shared_down_t)
    )
    a2, a0, z1, packed_o, shared_down_o, z3 = tie((a2, a0, z1, packed_o, shared_down_o, z3))
    experts = [(w_gate, w_up, w_down), (w_gate_o, w_up_o, w_down_o)]
    shared = [(shared_gate, shared_up, shared_down), (packed_o, packed_o, shared_down_o)]
    r3, d3, r1, d1 = right(z3), down(z3), right(z1), down(z1)
    out = run_experts([[own, r0, d0, a0], [z2, r2, d2, a2]], most, experts, shared)
    out, (r3, d3, r1, d1) = pin(out, (r3, d3, r1, d1))
    sum0, sum2 = out[:4], out[4:]
    a3, a1 = down(r3), right(d1)
    across0, across2 = down(sum0[3]), right(sum2[3])
    a3, a1, across0, across2, plain0, plain2 = tie(
        (a3, a1, across0, across2, sum0[2], sum2[1])
    )
    full0, full2 = add_rows(
        block, [[(sum0[1], 0), (across0, 0)], [(sum2[2], 0), (across2, 0)]]
    )
    sent0, sent2 = right(full0), down(full2)
    plain0, plain2 = down(plain0), right(plain2)
    out = run_experts([[z3, r3, d3, a3], [z1, r1, d1, a1]], most, experts, [], (full0,))
    out, (full0, full2, plain0, plain2) = pin(out, (sent0, sent2, plain0, plain2))
    sum3, sum1 = out[:4], out[4:]
    across3, across1 = down(sum3[3]), right(sum1[3])
    part2 = add_rows(block, [[(sum2[0], 0), (plain2, 0), (full2, 0)]])
    (part2,), (across3, across1) = pin(part2, (across3, across1))
    hop2 = far(part2, 1)
    full3, full1 = add_rows(
        block, [[(sum3[1], 0), (across3, 0)], [(sum1[2], 0), (across1, 0)]]
    )
    full3, plain3, plain1, full1 = tie((full3, sum3[2], sum1[1], full1))
    full3, plain3 = right(full3), down(plain3)
    full3, plain3, hop2, full1, plain1 = tie((full3, plain3, hop2, full1, plain1))
    full1, plain1 = down(full1), right(plain1)
    (part3,) = add_rows(block, [[(sum3[0], 0), (plain3, 0), (full3, 0), (hop2, 0)]])
    back3 = far(part3, 3)
    (part1,) = add_rows(block, [[(sum1[0], 0), (plain1, 0), (full1, 0)]])
    back1 = far(part1, 1)
    total = [(sum0[0], 0), (plain0, 0), (full0, 0), (back3, 0)]
    (total,) = add_rows(block, [total], jnp.float32)
    return add_rows(block, [[(total, 0), (back1, 0)]])[0]


def solution(mesh):
    sizes = dict(mesh.shape)

    def shards(*args):
        tokens, route_ids = args[0], args[1]
        slots = max(2, 2 * tokens.shape[0] * route_ids.shape[1] // (sizes["ex"] * sizes["ey"]))
        cube = sizes["ex"] == 2 * DOWN and sizes["ey"] == 4
        if cube and 4 * slots > tokens.shape[0]:
            return gather_all(*args)
        return exchange_slots(*args)

    in_specs = (
        P(("ex", "ey"), None),
        P(("ex", "ey"), None),
        P(("ex", "ey"), None),
        P(("ex", "ey"), None, None),
        P(("ex", "ey"), None, None),
        P(("ex", "ey"), None, None),
        P(None, "ex"),
        P(None, "ex"),
        P("ex", None),
    )
    out_specs = P(("ex", "ey"), None)
    return jax.shard_map(shards, mesh=mesh, in_specs=in_specs, out_specs=out_specs, check_vma=False)
```

```python
import functools

import jax
import jax.numpy as jnp
import numpy as np
from jax import lax
from jax.experimental import pallas as pl
from jax.experimental.pallas import tpu as pltpu
from jax.sharding import PartitionSpec as P


def swiglu(chosen, gate_weight, up_weight, down_weight):
    gate_act = jnp.dot(chosen, gate_weight, preferred_element_type=jnp.float32)
    up_act = jnp.dot(chosen, up_weight, preferred_element_type=jnp.float32)
    hidden = (jax.nn.silu(gate_act) * up_act).astype(jnp.bfloat16)
    return jnp.dot(hidden, down_weight, preferred_element_type=jnp.float32)


def shared_expert(tokens, shared_gate, shared_up, shared_down):
    gathered = lax.all_gather(tokens, "ex", axis=0, tiled=True)
    return lax.psum_scatter(
        swiglu(gathered, shared_gate, shared_up, shared_down).astype(jnp.bfloat16),
        "ex",
        scatter_dimension=0,
        tiled=True,
    ).astype(jnp.float32)


def exchange_slots(
    tokens, route_ids, route_weight, w_gate, w_up, w_down, shared_gate, shared_up, shared_down
):
    tok_rows = tokens.shape[0]
    top_count = route_ids.shape[1]
    width = tokens.shape[1]
    experts = lax.axis_size("ex") * lax.axis_size("ey")
    slot_most = max(2, 2 * tok_rows * top_count // experts)
    capacity = experts * slot_most
    flat_ids = route_ids.reshape(-1)
    onehot = (flat_ids[:, None] == jnp.arange(experts, dtype=jnp.int32)[None, :]).astype(jnp.int32)
    slot_rank = jnp.sum((jnp.cumsum(onehot, axis=0) - onehot) * onehot, axis=1)
    slot_place = flat_ids * slot_most + slot_rank
    matches = (slot_place[:, None] == jnp.arange(capacity, dtype=jnp.int32)[None, :]).astype(
        jnp.float32
    )
    matches = matches.reshape(tok_rows, top_count, capacity)
    placing = jnp.sum(matches, axis=1).astype(jnp.bfloat16)
    combine_mat = jnp.sum(matches * route_weight.astype(jnp.float32)[:, :, None], axis=1).astype(
        jnp.bfloat16
    )
    outgoing = jnp.einsum("tc,td->cd", placing, tokens, preferred_element_type=jnp.float32).astype(
        jnp.bfloat16
    )
    outgoing = outgoing.reshape(experts, slot_most, width)
    arrived = lax.all_to_all(outgoing, ("ex", "ey"), split_axis=0, concat_axis=0, tiled=True)
    layout = arrived.shape
    result = swiglu(arrived.reshape(-1, width), w_gate[0], w_up[0], w_down[0])
    produced = result.astype(jnp.bfloat16).reshape(layout)
    returned = lax.all_to_all(produced, ("ex", "ey"), split_axis=0, concat_axis=0, tiled=True)
    returned = returned.reshape(capacity, width)
    routed = jnp.dot(combine_mat, returned, preferred_element_type=jnp.float32)
    shared = shared_expert(tokens, shared_gate, shared_up, shared_down)
    return (shared + routed).astype(jnp.bfloat16)


PAIR, RIGHT, DOWN = 1, 2, 4
VMEM_LIMIT = 42 * 1024 * 1024


def swap(value, axis, mask):
    size = lax.axis_size(axis)
    return lax.ppermute(value, axis, [(i, i ^ mask) for i in range(size)])


def in_hbm(array):
    return pltpu.with_memory_space_constraint(array, pltpu.HBM)


def add_rows(*parts, dtype=jnp.bfloat16):
    total = parts[0].astype(jnp.float32)
    for part in parts[1:]:
        total = total + part.astype(jnp.float32)
    return total.astype(dtype)


LANES = 128


def tile_of(size, goal):
    return max(t for t in range(LANES, goal + 1, LANES) if size % t == 0)


def table_body(tokens, ids, rates, out):
    top, rows = ids.shape
    width = tokens.shape[1]
    expert = lax.broadcasted_iota(jnp.int32, (LANES, rows), 0)
    table = jnp.zeros((LANES, rows), jnp.float32)
    for k in range(top):
        hit = ids[k : k + 1, :] == expert
        table += jnp.where(hit, rates[k : k + 1, :].astype(jnp.float32), 0.0)
    out[:, :width] = tokens[...]
    out[:, width:] = table.T.astype(out.dtype)


def with_table(tokens, ids, rates):
    rows, width = tokens.shape
    return pl.pallas_call(
        table_body,
        out_shape=jax.ShapeDtypeStruct((rows, width + LANES), tokens.dtype),
    )(tokens, ids.T, rates.T)


def expert_body(dims, *refs):
    lows, block, most, width, hidden, shared_hidden, tile, span, ring = dims
    pieces_of = 4
    sides = len(lows) // pieces_of
    rows = pieces_of * block
    slots = pieces_of * most
    refs = list(refs)

    def take(number):
        out = refs[:number]
        del refs[:number]
        return out

    pieces = take(sides * pieces_of)
    (before_ref,) = take(1)
    experts = [take(3), take(3)]
    shared = [take(3), take(3)] if shared_hidden else []
    take(len(refs) - 15 - sides * pieces_of)
    outs = take(sides * pieces_of)
    held, chosen, gate, up, down, down_s, act, act_s, back, result = take(10)
    piece_sem, step_sem, span_sem, span_s_sem, out_sem = take(5)
    copy = pltpu.make_async_copy
    f32, bf16 = jnp.float32, jnp.bfloat16

    steps = [(part[0], part[1], low) for part, low in zip(shared, (0, shared_hidden))]
    steps += [
        (part[0].at[0], part[1].at[0], k * tile) for part in experts for k in range(hidden // tile)
    ]
    spans = width // span

    def piece_copy(k):
        rows_of = pl.ds(lows[k], block)
        return copy(pieces[k].at[rows_of], held.at[pl.ds(k * block, block), :], piece_sem.at[k])

    def step_copies(k):
        at = k % ring
        low = steps[k][2]
        gate_low = 0 if k < len(shared) else low
        return [
            copy(steps[k][0].at[:, pl.ds(gate_low, tile)], gate.at[at], step_sem.at[0, at]),
            copy(steps[k][1].at[:, pl.ds(low, tile)], up.at[at], step_sem.at[1, at]),
        ]

    def span_copies(k):
        at = k % ring
        columns = pl.ds(k * span, span)
        both = [
            copy(part[2].at[0, :, columns], down.at[at, e], span_sem.at[at, e])
            for e, part in enumerate(experts)
        ]
        return both + [
            copy(part[2].at[:, columns], down_s.at[at, e], span_s_sem.at[at, e])
            for e, part in enumerate(shared)
        ]

    def out_copy(side, piece, k):
        return copy(
            result.at[side, k, pl.ds(piece * block, block), :],
            outs[side * pieces_of + piece].at[:, pl.ds(k * span, span)],
            out_sem.at[side, piece, k],
        )

    def start(copies):
        for one in copies:
            one.start()

    def wait(copies):
        for one in copies:
            one.wait()

    start([piece_copy(k) for k in range(sides * pieces_of)])
    start(step_copies(0))

    ey = lax.axis_size("ey")
    ex = lax.axis_index("ex")
    me = ex * ey + lax.axis_index("ey")
    partner = (ex + PAIR - 2 * PAIR * (ex % (2 * PAIR))) * ey + lax.axis_index("ey")
    row = lax.broadcasted_iota(jnp.int32, (16, LANES), 0)
    lane = lax.broadcasted_iota(jnp.int32, (16, LANES), 1)
    pick = (lane == jnp.where(row == 0, me, partner)).astype(f32).astype(bf16)
    before = before_ref[:rows]
    base = before_ref[rows : rows + 16].astype(f32)[0:1]
    slot = lax.broadcasted_iota(jnp.int32, (slots, rows), 0).astype(f32)
    for side in range(sides):
        wait([piece_copy(k) for k in range(side * pieces_of, (side + 1) * pieces_of)])
        if side == 0:
            for k in range(1, ring):
                start(step_copies(k))
        low = side * rows
        table = held[low : low + rows, width : width + LANES]
        rate = lax.dot_general(
            pick, table, (((1,), (1,)), ((), ())), preferred_element_type=f32
        )
        named = (rate > 0).astype(f32)
        rank = jnp.dot(named.astype(bf16), before, preferred_element_type=f32)
        places = []
        for e in range(2):
            where = jnp.where(named[e : e + 1] > 0, rank[e : e + 1] + base, -1.0)
            place = slot == where
            back[side, :, e * slots : (e + 1) * slots] = jnp.where(
                place, rate[e : e + 1], 0.0
            ).T.astype(bf16)
            places.append(place.astype(f32).astype(bf16))
        picked = jnp.dot(
            jnp.concatenate(places, axis=0),
            held[low : low + rows, :width],
            preferred_element_type=f32,
        ).astype(bf16)
        for e in range(2):
            chosen[e, side * slots : (side + 1) * slots] = picked[e * slots : (e + 1) * slots]

    per = hidden // tile
    for k in range(len(steps)):
        wait(step_copies(k))
        e, at = divmod(k - len(shared), per)
        source = held[:rows, :width] if k < len(shared) else chosen[e]
        g = jnp.dot(source, gate[k % ring], preferred_element_type=f32)
        u = jnp.dot(source, up[k % ring], preferred_element_type=f32)
        h = (jax.nn.silu(g) * u).astype(bf16)
        if k < len(shared):
            act_s[k] = h
        else:
            act[e, :, at * tile : (at + 1) * tile] = h
        if k + ring < len(steps):
            start(step_copies(k + ring))
        elif k + ring - len(steps) < min(ring, spans):
            start(span_copies(k + ring - len(steps)))

    for k in range(spans):
        wait(span_copies(k))
        y = [
            jnp.dot(act[e], down[k % ring, e], preferred_element_type=f32).astype(bf16)
            for e in range(2)
        ]
        for side in range(sides):
            mine = [part[side * slots : (side + 1) * slots] for part in y]
            out = jnp.dot(back[side], jnp.concatenate(mine, axis=0), preferred_element_type=f32)
            if side == 0:
                for e in range(len(shared)):
                    out += jnp.dot(act_s[e], down_s[k % ring, e], preferred_element_type=f32)
            result[side, k] = out.astype(bf16)
            start([out_copy(side, piece, k) for piece in range(pieces_of)])
        if k + ring < spans:
            start(span_copies(k + ring))

    wait(
        [
            out_copy(side, piece, k)
            for side in range(sides)
            for piece in range(pieces_of)
            for k in range(spans)
        ]
    )


def run_experts(sides, block, most, experts, shared, after=()):
    wide = sides[0][0][0].shape[1]
    width, hidden = wide - LANES, experts[0][0].shape[2]
    shared_hidden = shared[0][0].shape[1] if shared else 0
    tile, span, ring = shared_hidden or tile_of(hidden, 256), tile_of(width, 1024), 3
    number, pieces_of = len(sides), len(sides[0])
    rows, slots = pieces_of * block, pieces_of * most
    lows = tuple(at * block for side in sides for _, at in side)
    dims = (lows, block, most, width, hidden, shared_hidden, tile, span, ring)
    bf16 = jnp.bfloat16
    vmem, sems = pltpu.VMEM, pltpu.SemaphoreType.DMA
    shared_rows = shared_hidden or 16
    scratch = [
        vmem((number * rows, wide), bf16),
        vmem((2, number * slots, width), bf16),
        vmem((ring, width, tile), bf16),
        vmem((ring, width, tile), bf16),
        vmem((ring, 2, hidden, span), bf16),
        vmem((ring, 2, shared_rows, span), bf16),
        vmem((2, number * slots, hidden), bf16),
        vmem((2, rows, max(shared_rows, LANES)), bf16),
        vmem((number, rows, 2 * slots), bf16),
        vmem((number, width // span, rows, span), bf16),
        sems((number * pieces_of,)),
        sems((2, ring)),
        sems((ring, 2)),
        sems((ring, 2)),
        sems((number, pieces_of, width // span)),
    ]
    token = np.arange(rows)
    before = (token[:, None] < token) & (token[:, None] // block == token // block)
    base = np.broadcast_to(token // block * most, (16, rows))
    before = jnp.asarray(np.concatenate([before, base], axis=0), bf16)
    operands = [part for side in sides for part, _ in side] + [before]
    operands += [part for weights in (*experts, *shared) for part in weights]
    moved = 2 * (sum(part.size for part in operands) + number * rows * width)
    flops = 2 * number * (6 * slots * width * hidden + 4 * rows * slots * width)
    flops += 12 * rows * width * shared_hidden
    operands += after
    operands = [part if part is before else in_hbm(part) for part in operands]
    return pl.pallas_call(
        functools.partial(expert_body, dims),
        out_shape=[pltpu.HBM((block, width), bf16)] * (number * pieces_of),
        in_specs=[
            pl.BlockSpec(memory_space=pltpu.VMEM if part is before else pl.ANY) for part in operands
        ],
        out_specs=[pl.BlockSpec(memory_space=pl.ANY)] * (number * pieces_of),
        scratch_shapes=scratch,
        compiler_params=pltpu.CompilerParams(vmem_limit_bytes=VMEM_LIMIT),
        cost_estimate=pl.CostEstimate(flops=flops, bytes_accessed=moved, transcendentals=0),
    )(*operands)


def pin(done, moving):
    count = len(done)
    both = lax.optimization_barrier((*done, *moving))
    return list(both[:count]), list(both[count:])


def gather_all(
    tokens, route_ids, route_weight, w_gate, w_up, w_down, shared_gate, shared_up, shared_down
):
    block = tokens.shape[0]
    experts = lax.axis_size("ex") * lax.axis_size("ey")
    most = max(2, 2 * block * route_ids.shape[1] // experts)
    own = with_table(tokens, route_ids, route_weight)
    def right(value):
        return swap(value, "ex", RIGHT)

    def down(value):
        return swap(value, "ex", DOWN)

    def pair(value):
        return swap(value, "ex", PAIR)

    def far(value, mask):
        return swap(value, "ey", mask)

    tie = lax.optimization_barrier
    z2, r0, d0, w_gate_o, w_up_o = far(own, 2), right(own), down(own), pair(w_gate), pair(w_up)
    packed = jnp.concatenate([shared_gate, shared_up], axis=1)
    z2, r0, d0, w_gate_o, w_up_o, w_down_t, packed = tie(
        (z2, r0, d0, w_gate_o, w_up_o, w_down, packed)
    )
    r2, d2, z3, w_down_o = right(z2), down(z2), far(z2, 1), pair(w_down_t)
    r0, r2, d2, z3, w_down_o, packed, shared_down_t, own_t = tie(
        (r0, r2, d2, z3, w_down_o, packed, shared_down, own)
    )
    a2, a0, z1, packed_o, shared_down_o = (
        right(d2), down(r0), far(own_t, 1), pair(packed), pair(shared_down_t)
    )
    a2, a0, z1, packed_o, shared_down_o, z3 = tie((a2, a0, z1, packed_o, shared_down_o, z3))
    experts = [(w_gate, w_up, w_down), (w_gate_o, w_up_o, w_down_o)]
    shared = [(shared_gate, shared_up, shared_down), (packed_o, packed_o, shared_down_o)]
    pair31 = jnp.concatenate([z3, z1], axis=0)
    r31, d31, a3, a1 = right(pair31), down(pair31), far(a2, 1), far(a0, 1)
    sides = [[(own, 0), (r0, 0), (d0, 0), (a0, 0)], [(z2, 0), (r2, 0), (d2, 0), (a2, 0)]]
    out = run_experts(sides, block, most, experts, shared)
    out, (r31, d31, a3, a1) = pin(out, (r31, d31, a3, a1))
    sum0, sum2 = out[:4], out[4:]
    sent0, sent2, plain0, plain2 = down(sum0[3]), right(sum2[3]), down(sum0[2]), right(sum2[1])
    sides = [[(z3, 0), (r31, 0), (d31, 0), (a3, 0)], [(z1, 0), (r31, 1), (d31, 1), (a1, 0)]]
    out = run_experts(sides, block, most, experts, [], (sum0[0],))
    out, (across0, across2, plain0, plain2) = pin(out, (sent0, sent2, plain0, plain2))
    sum3, sum1 = out[:4], out[4:]
    across3, across1 = down(sum3[3]), right(sum1[3])
    full0, full2 = add_rows(sum0[1], across0), add_rows(sum2[2], across2)
    full0, full2 = right(full0), down(full2)
    across3, across1, full0, full2, plain3, plain1 = tie(
        (across3, across1, full0, full2, sum3[2], sum1[1])
    )
    hop2 = far(add_rows(sum2[0], plain2, full2), 1)
    full3, full1 = add_rows(sum3[1], across3), add_rows(sum1[2], across1)
    full3, plain3, plain1, full1 = tie((full3, plain3, plain1, full1))
    full3, plain3 = right(full3), down(plain3)
    full3, plain3, hop2, full1, plain1 = tie((full3, plain3, hop2, full1, plain1))
    full1, plain1 = down(full1), right(plain1)
    part3 = add_rows(sum3[0], plain3, full3, hop2)
    back3 = far(part3, 3)
    part1 = add_rows(sum1[0], plain1, full1)
    back1 = far(part1, 1)
    total = add_rows(sum0[0], plain0, full0, back3, dtype=jnp.float32)
    return add_rows(total, back1)


def solution(mesh):
    sizes = dict(mesh.shape)

    def shards(*args):
        tokens, route_ids = args[0], args[1]
        slots = max(2, 2 * tokens.shape[0] * route_ids.shape[1] // (sizes["ex"] * sizes["ey"]))
        cube = sizes["ex"] == 2 * DOWN and sizes["ey"] == 4
        if cube and 4 * slots > tokens.shape[0]:
            return gather_all(*args)
        return exchange_slots(*args)

    in_specs = (
        P(("ex", "ey"), None),
        P(("ex", "ey"), None),
        P(("ex", "ey"), None),
        P(("ex", "ey"), None, None),
        P(("ex", "ey"), None, None),
        P(("ex", "ey"), None, None),
        P(None, "ex"),
        P(None, "ex"),
        P("ex", None),
    )
    out_specs = P(("ex", "ey"), None)
    return jax.shard_map(shards, mesh=mesh, in_specs=in_specs, out_specs=out_specs, check_vma=False)
```

```python
import functools

import jax
import jax.numpy as jnp
import numpy as np
from jax import lax
from jax.experimental import pallas as pl
from jax.experimental.pallas import tpu as pltpu
from jax.sharding import PartitionSpec as P


def swiglu(chosen, gate_weight, up_weight, down_weight):
    gate_act = jnp.dot(chosen, gate_weight, preferred_element_type=jnp.float32)
    up_act = jnp.dot(chosen, up_weight, preferred_element_type=jnp.float32)
    hidden = (jax.nn.silu(gate_act) * up_act).astype(jnp.bfloat16)
    return jnp.dot(hidden, down_weight, preferred_element_type=jnp.float32)


def shared_expert(tokens, shared_gate, shared_up, shared_down):
    gathered = lax.all_gather(tokens, "ex", axis=0, tiled=True)
    return lax.psum_scatter(
        swiglu(gathered, shared_gate, shared_up, shared_down).astype(jnp.bfloat16),
        "ex",
        scatter_dimension=0,
        tiled=True,
    ).astype(jnp.float32)


def exchange_slots(
    tokens, route_ids, route_weight, w_gate, w_up, w_down, shared_gate, shared_up, shared_down
):
    tok_rows = tokens.shape[0]
    top_count = route_ids.shape[1]
    width = tokens.shape[1]
    experts = lax.axis_size("ex") * lax.axis_size("ey")
    slot_most = max(2, 2 * tok_rows * top_count // experts)
    capacity = experts * slot_most
    flat_ids = route_ids.reshape(-1)
    onehot = (flat_ids[:, None] == jnp.arange(experts, dtype=jnp.int32)[None, :]).astype(jnp.int32)
    slot_rank = jnp.sum((jnp.cumsum(onehot, axis=0) - onehot) * onehot, axis=1)
    slot_place = flat_ids * slot_most + slot_rank
    matches = (slot_place[:, None] == jnp.arange(capacity, dtype=jnp.int32)[None, :]).astype(
        jnp.float32
    )
    matches = matches.reshape(tok_rows, top_count, capacity)
    placing = jnp.sum(matches, axis=1).astype(jnp.bfloat16)
    combine_mat = jnp.sum(matches * route_weight.astype(jnp.float32)[:, :, None], axis=1).astype(
        jnp.bfloat16
    )
    outgoing = jnp.einsum("tc,td->cd", placing, tokens, preferred_element_type=jnp.float32).astype(
        jnp.bfloat16
    )
    outgoing = outgoing.reshape(experts, slot_most, width)
    arrived = lax.all_to_all(outgoing, ("ex", "ey"), split_axis=0, concat_axis=0, tiled=True)
    layout = arrived.shape
    result = swiglu(arrived.reshape(-1, width), w_gate[0], w_up[0], w_down[0])
    produced = result.astype(jnp.bfloat16).reshape(layout)
    returned = lax.all_to_all(produced, ("ex", "ey"), split_axis=0, concat_axis=0, tiled=True)
    returned = returned.reshape(capacity, width)
    routed = jnp.dot(combine_mat, returned, preferred_element_type=jnp.float32)
    shared = shared_expert(tokens, shared_gate, shared_up, shared_down)
    return (shared + routed).astype(jnp.bfloat16)


PAIR, RIGHT, DOWN = 1, 2, 4
VMEM_LIMIT = 42 * 1024 * 1024


def swap(value, axis, mask):
    size = lax.axis_size(axis)
    return lax.ppermute(value, axis, [(i, i ^ mask) for i in range(size)])


def in_hbm(array):
    return pltpu.with_memory_space_constraint(array, pltpu.HBM)


def add_rows(*parts, dtype=jnp.bfloat16):
    total = parts[0].astype(jnp.float32)
    for part in parts[1:]:
        total = total + part.astype(jnp.float32)
    return total.astype(dtype)


LANES = 128


def tile_of(size, goal):
    return max(t for t in range(LANES, goal + 1, LANES) if size % t == 0)


def table_body(tokens, ids, rates, out):
    top, rows = ids.shape
    width = tokens.shape[1]
    expert = lax.broadcasted_iota(jnp.int32, (LANES, rows), 0)
    table = jnp.zeros((LANES, rows), jnp.float32)
    for k in range(top):
        hit = ids[k : k + 1, :] == expert
        table += jnp.where(hit, rates[k : k + 1, :].astype(jnp.float32), 0.0)
    out[:, :width] = tokens[...]
    out[:, width:] = table.T.astype(out.dtype)


def with_table(tokens, ids, rates):
    rows, width = tokens.shape
    return pl.pallas_call(
        table_body,
        out_shape=jax.ShapeDtypeStruct((rows, width + LANES), tokens.dtype),
    )(tokens, ids.T, rates.T)


def expert_body(dims, *refs):
    lows, packed, block, most, width, hidden, shared_hidden, tile, span, ring = dims
    pieces_of = 4
    sides = len(lows) // pieces_of
    rows = pieces_of * block
    slots = pieces_of * most
    refs = list(refs)

    def take(number):
        out = refs[:number]
        del refs[:number]
        return out

    pieces = take(sides * pieces_of)
    (before_ref,) = take(1)
    experts = [take(3), take(3)]
    shared = [take(3), take(3)] if shared_hidden else []
    outs_of = pieces_of if packed else sides * pieces_of
    take(len(refs) - 15 - outs_of)
    outs = take(outs_of)
    held, chosen, gate, up, down, down_s, act, act_s, back, result = take(10)
    piece_sem, step_sem, span_sem, span_s_sem, out_sem = take(5)
    copy = pltpu.make_async_copy
    f32, bf16 = jnp.float32, jnp.bfloat16

    steps = [(part[0], part[1], low) for part, low in zip(shared, (0, shared_hidden))]
    steps += [
        (part[0].at[0], part[1].at[0], k * tile) for part in experts for k in range(hidden // tile)
    ]
    spans = width // span

    def piece_copy(k):
        rows_of = pl.ds(lows[k], block)
        return copy(pieces[k].at[rows_of], held.at[pl.ds(k * block, block), :], piece_sem.at[k])

    def step_copies(k):
        at = k % ring
        low = steps[k][2]
        gate_low = 0 if k < len(shared) else low
        return [
            copy(steps[k][0].at[:, pl.ds(gate_low, tile)], gate.at[at], step_sem.at[0, at]),
            copy(steps[k][1].at[:, pl.ds(low, tile)], up.at[at], step_sem.at[1, at]),
        ]

    def span_copies(k):
        at = k % ring
        columns = pl.ds(k * span, span)
        both = [
            copy(part[2].at[0, :, columns], down.at[at, e], span_sem.at[at, e])
            for e, part in enumerate(experts)
        ]
        return both + [
            copy(part[2].at[:, columns], down_s.at[at, e], span_s_sem.at[at, e])
            for e, part in enumerate(shared)
        ]

    def out_copy(side, piece, k):
        columns = pl.ds(k * span, span)
        if packed:
            out = outs[piece].at[pl.ds(side * block, block), columns]
        else:
            out = outs[side * pieces_of + piece].at[:, columns]
        rows_of = pl.ds(piece * block, block)
        return copy(result.at[side, k, rows_of, :], out, out_sem.at[side, piece, k])

    def start(copies):
        for one in copies:
            one.start()

    def wait(copies):
        for one in copies:
            one.wait()

    start([piece_copy(k) for k in range(sides * pieces_of)])
    start(step_copies(0))

    ey = lax.axis_size("ey")
    ex = lax.axis_index("ex")
    me = ex * ey + lax.axis_index("ey")
    partner = (ex + PAIR - 2 * PAIR * (ex % (2 * PAIR))) * ey + lax.axis_index("ey")
    row = lax.broadcasted_iota(jnp.int32, (16, LANES), 0)
    lane = lax.broadcasted_iota(jnp.int32, (16, LANES), 1)
    pick = (lane == jnp.where(row == 0, me, partner)).astype(f32).astype(bf16)
    before = before_ref[:rows]
    base = before_ref[rows : rows + 16].astype(f32)[0:1]
    slot = lax.broadcasted_iota(jnp.int32, (slots, rows), 0).astype(f32)
    for side in range(sides):
        wait([piece_copy(k) for k in range(side * pieces_of, (side + 1) * pieces_of)])
        if side == 0:
            for k in range(1, ring):
                start(step_copies(k))
        low = side * rows
        table = held[low : low + rows, width : width + LANES]
        rate = lax.dot_general(
            pick, table, (((1,), (1,)), ((), ())), preferred_element_type=f32
        )
        named = (rate > 0).astype(f32)
        rank = jnp.dot(named.astype(bf16), before, preferred_element_type=f32)
        places = []
        for e in range(2):
            where = jnp.where(named[e : e + 1] > 0, rank[e : e + 1] + base, -1.0)
            place = slot == where
            back[side, :, e * slots : (e + 1) * slots] = jnp.where(
                place, rate[e : e + 1], 0.0
            ).T.astype(bf16)
            places.append(place.astype(f32).astype(bf16))
        picked = jnp.dot(
            jnp.concatenate(places, axis=0),
            held[low : low + rows, :width],
            preferred_element_type=f32,
        ).astype(bf16)
        for e in range(2):
            chosen[e, side * slots : (side + 1) * slots] = picked[e * slots : (e + 1) * slots]

    per = hidden // tile
    for k in range(len(steps)):
        wait(step_copies(k))
        e, at = divmod(k - len(shared), per)
        source = held[:rows, :width] if k < len(shared) else chosen[e]
        g = jnp.dot(source, gate[k % ring], preferred_element_type=f32)
        u = jnp.dot(source, up[k % ring], preferred_element_type=f32)
        h = (jax.nn.silu(g) * u).astype(bf16)
        if k < len(shared):
            act_s[k] = h
        else:
            act[e, :, at * tile : (at + 1) * tile] = h
        if k + ring < len(steps):
            start(step_copies(k + ring))
        elif k + ring - len(steps) < min(ring, spans):
            start(span_copies(k + ring - len(steps)))

    for k in range(spans):
        wait(span_copies(k))
        y = [
            jnp.dot(act[e], down[k % ring, e], preferred_element_type=f32).astype(bf16)
            for e in range(2)
        ]
        for side in range(sides):
            mine = [part[side * slots : (side + 1) * slots] for part in y]
            out = jnp.dot(back[side], jnp.concatenate(mine, axis=0), preferred_element_type=f32)
            if side == 0:
                for e in range(len(shared)):
                    out += jnp.dot(act_s[e], down_s[k % ring, e], preferred_element_type=f32)
            result[side, k] = out.astype(bf16)
            start([out_copy(side, piece, k) for piece in range(pieces_of)])
        if k + ring < spans:
            start(span_copies(k + ring))

    wait(
        [
            out_copy(side, piece, k)
            for side in range(sides)
            for piece in range(pieces_of)
            for k in range(spans)
        ]
    )


def run_experts(sides, block, most, experts, shared, packed, after=()):
    wide = sides[0][0][0].shape[1]
    width, hidden = wide - LANES, experts[0][0].shape[2]
    shared_hidden = shared[0][0].shape[1] if shared else 0
    tile, span, ring = shared_hidden or tile_of(hidden, 256), tile_of(width, 1024), 3
    number, pieces_of = len(sides), len(sides[0])
    rows, slots = pieces_of * block, pieces_of * most
    lows = tuple(at * block for side in sides for _, at in side)
    dims = (lows, packed, block, most, width, hidden, shared_hidden, tile, span, ring)
    bf16 = jnp.bfloat16
    vmem, sems = pltpu.VMEM, pltpu.SemaphoreType.DMA
    shared_rows = shared_hidden or 16
    scratch = [
        vmem((number * rows, wide), bf16),
        vmem((2, number * slots, width), bf16),
        vmem((ring, width, tile), bf16),
        vmem((ring, width, tile), bf16),
        vmem((ring, 2, hidden, span), bf16),
        vmem((ring, 2, shared_rows, span), bf16),
        vmem((2, number * slots, hidden), bf16),
        vmem((2, rows, max(shared_rows, LANES)), bf16),
        vmem((number, rows, 2 * slots), bf16),
        vmem((number, width // span, rows, span), bf16),
        sems((number * pieces_of,)),
        sems((2, ring)),
        sems((ring, 2)),
        sems((ring, 2)),
        sems((number, pieces_of, width // span)),
    ]
    token = np.arange(rows)
    before = (token[:, None] < token) & (token[:, None] // block == token // block)
    base = np.broadcast_to(token // block * most, (16, rows))
    before = jnp.asarray(np.concatenate([before, base], axis=0), bf16)
    operands = [part for side in sides for part, _ in side] + [before]
    operands += [part for weights in (*experts, *shared) for part in weights]
    moved = 2 * (sum(part.size for part in operands) + number * rows * width)
    flops = 2 * number * (6 * slots * width * hidden + 4 * rows * slots * width)
    flops += 12 * rows * width * shared_hidden
    operands += after
    operands = [part if part is before else in_hbm(part) for part in operands]
    return pl.pallas_call(
        functools.partial(expert_body, dims),
        out_shape=[pltpu.HBM((block * number, width), bf16)] * pieces_of
        if packed
        else [pltpu.HBM((block, width), bf16)] * (number * pieces_of),
        in_specs=[
            pl.BlockSpec(memory_space=pltpu.VMEM if part is before else pl.ANY) for part in operands
        ],
        out_specs=[pl.BlockSpec(memory_space=pl.ANY)] * (pieces_of * (1 if packed else number)),
        scratch_shapes=scratch,
        compiler_params=pltpu.CompilerParams(vmem_limit_bytes=VMEM_LIMIT),
        cost_estimate=pl.CostEstimate(flops=flops, bytes_accessed=moved, transcendentals=0),
    )(*operands)


def pin(done, moving):
    count = len(done)
    both = lax.optimization_barrier((*done, *moving))
    return list(both[:count]), list(both[count:])


def gather_all(
    tokens, route_ids, route_weight, w_gate, w_up, w_down, shared_gate, shared_up, shared_down
):
    block = tokens.shape[0]
    experts = lax.axis_size("ex") * lax.axis_size("ey")
    most = max(2, 2 * block * route_ids.shape[1] // experts)
    own = with_table(tokens, route_ids, route_weight)
    def right(value):
        return swap(value, "ex", RIGHT)

    def down(value):
        return swap(value, "ex", DOWN)

    def pair(value):
        return swap(value, "ex", PAIR)

    def far(value, mask):
        return swap(value, "ey", mask)

    tie = lax.optimization_barrier
    z2, r0, d0, w_gate_o, w_up_o = far(own, 2), right(own), down(own), pair(w_gate), pair(w_up)
    packed = jnp.concatenate([shared_gate, shared_up], axis=1)
    z2, r0, d0, w_gate_o, w_up_o, w_down_t, packed = tie(
        (z2, r0, d0, w_gate_o, w_up_o, w_down, packed)
    )
    r2, d2, z3, w_down_o = right(z2), down(z2), far(z2, 1), pair(w_down_t)
    r0, r2, d2, z3, w_down_o, packed, shared_down_t, own_t = tie(
        (r0, r2, d2, z3, w_down_o, packed, shared_down, own)
    )
    a2, a0, z1, packed_o, shared_down_o = (
        right(d2), down(r0), far(own_t, 1), pair(packed), pair(shared_down_t)
    )
    a2, a0, z1, packed_o, shared_down_o, z3 = tie((a2, a0, z1, packed_o, shared_down_o, z3))
    experts = [(w_gate, w_up, w_down), (w_gate_o, w_up_o, w_down_o)]
    shared = [(shared_gate, shared_up, shared_down), (packed_o, packed_o, shared_down_o)]
    pair31 = jnp.concatenate([z3, z1], axis=0)
    r31, d31, a3, a1 = right(pair31), down(pair31), far(a2, 1), far(a0, 1)
    sides = [[(own, 0), (r0, 0), (d0, 0), (a0, 0)], [(z2, 0), (r2, 0), (d2, 0), (a2, 0)]]
    out = run_experts(sides, block, most, experts, shared, True)
    out, (r31, d31, a3, a1) = pin(out, (r31, d31, a3, a1))
    sums = out[0]
    from_right, from_down, from_far = right(out[1]), down(out[2]), far(out[3], 1)
    sides = [[(z1, 0), (r31, 1), (d31, 1), (a1, 0)], [(z3, 0), (r31, 0), (d31, 0), (a3, 0)]]
    out = run_experts(sides, block, most, experts, [], False, (sums,))
    out, (from_right, from_down, from_far) = pin(out, (from_right, from_down, from_far))
    sum1, sum3 = out[:4], out[4:]
    across3 = down(add_rows(sum3[3], from_far[block:]))
    across1 = right(add_rows(sum1[3], from_far[:block]))
    hop2 = far(add_rows(sums[block:], from_right[block:], from_down[block:]), 1)
    across3, across1, hop2, plain3, plain1 = tie((across3, across1, hop2, sum3[2], sum1[1]))
    full3, full1 = add_rows(sum3[1], across3), add_rows(sum1[2], across1)
    full3, plain3, plain1, full1 = tie((full3, plain3, plain1, full1))
    full3, plain3 = right(full3), down(plain3)
    full3, plain3, full1, plain1 = tie((full3, plain3, full1, plain1))
    full1, plain1 = down(full1), right(plain1)
    part3 = add_rows(sum3[0], plain3, full3, hop2)
    back3 = far(part3, 3)
    part1 = add_rows(sum1[0], plain1, full1)
    back1 = far(part1, 1)
    total = add_rows(sums[:block], from_right[:block], from_down[:block], back3, dtype=jnp.float32)
    return add_rows(total, back1)


def solution(mesh):
    sizes = dict(mesh.shape)

    def shards(*args):
        tokens, route_ids = args[0], args[1]
        slots = max(2, 2 * tokens.shape[0] * route_ids.shape[1] // (sizes["ex"] * sizes["ey"]))
        cube = sizes["ex"] == 2 * DOWN and sizes["ey"] == 4
        if cube and 4 * slots > tokens.shape[0]:
            return gather_all(*args)
        return exchange_slots(*args)

    in_specs = (
        P(("ex", "ey"), None),
        P(("ex", "ey"), None),
        P(("ex", "ey"), None),
        P(("ex", "ey"), None, None),
        P(("ex", "ey"), None, None),
        P(("ex", "ey"), None, None),
        P(None, "ex"),
        P(None, "ex"),
        P("ex", None),
    )
    out_specs = P(("ex", "ey"), None)
    return jax.shard_map(shards, mesh=mesh, in_specs=in_specs, out_specs=out_specs, check_vma=False)
```

```python
import functools

import jax
import jax.numpy as jnp
import numpy as np
from jax import lax
from jax.experimental import pallas as pl
from jax.experimental.pallas import tpu as pltpu
from jax.sharding import PartitionSpec as P


def swiglu(chosen, gate_weight, up_weight, down_weight):
    gate_act = jnp.dot(chosen, gate_weight, preferred_element_type=jnp.float32)
    up_act = jnp.dot(chosen, up_weight, preferred_element_type=jnp.float32)
    hidden = (jax.nn.silu(gate_act) * up_act).astype(jnp.bfloat16)
    return jnp.dot(hidden, down_weight, preferred_element_type=jnp.float32)


def shared_expert(tokens, shared_gate, shared_up, shared_down):
    gathered = lax.all_gather(tokens, "ex", axis=0, tiled=True)
    return lax.psum_scatter(
        swiglu(gathered, shared_gate, shared_up, shared_down).astype(jnp.bfloat16),
        "ex",
        scatter_dimension=0,
        tiled=True,
    ).astype(jnp.float32)


def exchange_slots(
    tokens, route_ids, route_weight, w_gate, w_up, w_down, shared_gate, shared_up, shared_down
):
    tok_rows = tokens.shape[0]
    top_count = route_ids.shape[1]
    width = tokens.shape[1]
    experts = lax.axis_size("ex") * lax.axis_size("ey")
    slot_most = max(2, 2 * tok_rows * top_count // experts)
    capacity = experts * slot_most
    flat_ids = route_ids.reshape(-1)
    onehot = (flat_ids[:, None] == jnp.arange(experts, dtype=jnp.int32)[None, :]).astype(jnp.int32)
    slot_rank = jnp.sum((jnp.cumsum(onehot, axis=0) - onehot) * onehot, axis=1)
    slot_place = flat_ids * slot_most + slot_rank
    matches = (slot_place[:, None] == jnp.arange(capacity, dtype=jnp.int32)[None, :]).astype(
        jnp.float32
    )
    matches = matches.reshape(tok_rows, top_count, capacity)
    placing = jnp.sum(matches, axis=1).astype(jnp.bfloat16)
    combine_mat = jnp.sum(matches * route_weight.astype(jnp.float32)[:, :, None], axis=1).astype(
        jnp.bfloat16
    )
    outgoing = jnp.einsum("tc,td->cd", placing, tokens, preferred_element_type=jnp.float32).astype(
        jnp.bfloat16
    )
    outgoing = outgoing.reshape(experts, slot_most, width)
    arrived = lax.all_to_all(outgoing, ("ex", "ey"), split_axis=0, concat_axis=0, tiled=True)
    layout = arrived.shape
    result = swiglu(arrived.reshape(-1, width), w_gate[0], w_up[0], w_down[0])
    produced = result.astype(jnp.bfloat16).reshape(layout)
    returned = lax.all_to_all(produced, ("ex", "ey"), split_axis=0, concat_axis=0, tiled=True)
    returned = returned.reshape(capacity, width)
    routed = jnp.dot(combine_mat, returned, preferred_element_type=jnp.float32)
    shared = shared_expert(tokens, shared_gate, shared_up, shared_down)
    return (shared + routed).astype(jnp.bfloat16)


PAIR, RIGHT, DOWN = 1, 2, 4
VMEM_LIMIT = 39 * 1024 * 1024


def swap(value, axis, mask):
    size = lax.axis_size(axis)
    return lax.ppermute(value, axis, [(i, i ^ mask) for i in range(size)])


def in_hbm(array):
    return pltpu.with_memory_space_constraint(array, pltpu.HBM)


def add_rows(*parts, dtype=jnp.bfloat16):
    total = parts[0].astype(jnp.float32)
    for part in parts[1:]:
        total = total + part.astype(jnp.float32)
    return total.astype(dtype)


LANES = 128


def tile_of(size, goal):
    return max(t for t in range(LANES, goal + 1, LANES) if size % t == 0)


def table_body(tokens, ids, rates, out):
    top, rows = ids.shape
    width = tokens.shape[1]
    expert = lax.broadcasted_iota(jnp.int32, (LANES, rows), 0)
    table = jnp.zeros((LANES, rows), jnp.float32)
    for k in range(top):
        hit = ids[k : k + 1, :] == expert
        table += jnp.where(hit, rates[k : k + 1, :].astype(jnp.float32), 0.0)
    out[:, :width] = tokens[...]
    out[:, width:] = table.T.astype(out.dtype)


def with_table(tokens, ids, rates):
    rows, width = tokens.shape
    return pl.pallas_call(
        table_body,
        out_shape=jax.ShapeDtypeStruct((rows, width + LANES), tokens.dtype),
    )(tokens, ids.T, rates.T)


def expert_body(dims, *refs):
    lows, packed, block, most, width, hidden, shared_hidden, tile, span, ring = dims
    pieces_of = 4
    sides = len(lows) // pieces_of
    rows = pieces_of * block
    slots = pieces_of * most
    refs = list(refs)

    def take(number):
        out = refs[:number]
        del refs[:number]
        return out

    pieces = take(sides * pieces_of)
    (before_ref,) = take(1)
    experts = [take(3), take(3)]
    shared = [take(3), take(3)] if shared_hidden else []
    outs_of = pieces_of if packed else sides * pieces_of
    take(len(refs) - 15 - outs_of)
    outs = take(outs_of)
    held, chosen, gate, up, down, down_s, act, act_s, back, result = take(10)
    piece_sem, step_sem, span_sem, span_s_sem, out_sem = take(5)
    copy = pltpu.make_async_copy
    f32, bf16 = jnp.float32, jnp.bfloat16

    steps = [(part[0], part[1], low) for part, low in zip(shared, (0, shared_hidden))]
    steps += [
        (part[0].at[0], part[1].at[0], k * tile) for part in experts for k in range(hidden // tile)
    ]
    spans = width // span

    def piece_copy(k):
        rows_of = pl.ds(lows[k], block)
        return copy(pieces[k].at[rows_of], held.at[pl.ds(k * block, block), :], piece_sem.at[k])

    def step_copies(k):
        at = k % ring
        low = steps[k][2]
        gate_low = 0 if k < len(shared) else low
        return [
            copy(steps[k][0].at[:, pl.ds(gate_low, tile)], gate.at[at], step_sem.at[0, at]),
            copy(steps[k][1].at[:, pl.ds(low, tile)], up.at[at], step_sem.at[1, at]),
        ]

    def span_copies(k):
        at = k % ring
        columns = pl.ds(k * span, span)
        both = [
            copy(part[2].at[0, :, columns], down.at[at, e], span_sem.at[at, e])
            for e, part in enumerate(experts)
        ]
        return both + [
            copy(part[2].at[:, columns], down_s.at[at, e], span_s_sem.at[at, e])
            for e, part in enumerate(shared)
        ]

    def out_copy(side, piece, k):
        columns = pl.ds(k * span, span)
        if packed:
            out = outs[piece].at[pl.ds(side * block, block), columns]
        else:
            out = outs[side * pieces_of + piece].at[:, columns]
        rows_of = pl.ds(piece * block, block)
        return copy(result.at[side, k, rows_of, :], out, out_sem.at[side, piece, k])

    def start(copies):
        for one in copies:
            one.start()

    def wait(copies):
        for one in copies:
            one.wait()

    start([piece_copy(k) for k in range(sides * pieces_of)])
    start(step_copies(0))

    ey = lax.axis_size("ey")
    ex = lax.axis_index("ex")
    me = ex * ey + lax.axis_index("ey")
    partner = (ex + PAIR - 2 * PAIR * (ex % (2 * PAIR))) * ey + lax.axis_index("ey")
    row = lax.broadcasted_iota(jnp.int32, (16, LANES), 0)
    lane = lax.broadcasted_iota(jnp.int32, (16, LANES), 1)
    pick = (lane == jnp.where(row == 0, me, partner)).astype(f32).astype(bf16)
    before = before_ref[:rows]
    base = before_ref[rows : rows + 16].astype(f32)[0:1]
    slot = lax.broadcasted_iota(jnp.int32, (slots, rows), 0).astype(f32)
    for side in range(sides):
        wait([piece_copy(k) for k in range(side * pieces_of, (side + 1) * pieces_of)])
        if side == 0:
            for k in range(1, ring):
                start(step_copies(k))
        low = side * rows
        table = held[low : low + rows, width : width + LANES]
        rate = lax.dot_general(
            pick, table, (((1,), (1,)), ((), ())), preferred_element_type=f32
        )
        named = (rate > 0).astype(f32)
        rank = jnp.dot(named.astype(bf16), before, preferred_element_type=f32)
        places = []
        for e in range(2):
            where = jnp.where(named[e : e + 1] > 0, rank[e : e + 1] + base, -1.0)
            place = slot == where
            back[side, :, e * slots : (e + 1) * slots] = jnp.where(
                place, rate[e : e + 1], 0.0
            ).T.astype(bf16)
            places.append(place.astype(f32).astype(bf16))
        picked = jnp.dot(
            jnp.concatenate(places, axis=0),
            held[low : low + rows, :width],
            preferred_element_type=f32,
        ).astype(bf16)
        for e in range(2):
            chosen[e, side * slots : (side + 1) * slots] = picked[e * slots : (e + 1) * slots]

    per = hidden // tile
    for k in range(len(steps)):
        wait(step_copies(k))
        e, at = divmod(k - len(shared), per)
        source = held[:rows, :width] if k < len(shared) else chosen[e]
        g = jnp.dot(source, gate[k % ring], preferred_element_type=f32)
        u = jnp.dot(source, up[k % ring], preferred_element_type=f32)
        h = (jax.nn.silu(g) * u).astype(bf16)
        if k < len(shared):
            act_s[k] = h
        else:
            act[e, :, at * tile : (at + 1) * tile] = h
        if k + ring < len(steps):
            start(step_copies(k + ring))
        elif k + ring - len(steps) < min(ring, spans):
            start(span_copies(k + ring - len(steps)))

    for k in range(spans):
        wait(span_copies(k))
        y = [
            jnp.dot(act[e], down[k % ring, e], preferred_element_type=f32).astype(bf16)
            for e in range(2)
        ]
        for side in range(sides):
            mine = [part[side * slots : (side + 1) * slots] for part in y]
            out = jnp.dot(back[side], jnp.concatenate(mine, axis=0), preferred_element_type=f32)
            if side == 0:
                for e in range(len(shared)):
                    out += jnp.dot(act_s[e], down_s[k % ring, e], preferred_element_type=f32)
            result[side, k] = out.astype(bf16)
            start([out_copy(side, piece, k) for piece in range(pieces_of)])
        if k + ring < spans:
            start(span_copies(k + ring))

    wait(
        [
            out_copy(side, piece, k)
            for side in range(sides)
            for piece in range(pieces_of)
            for k in range(spans)
        ]
    )


def run_experts(sides, block, most, experts, shared, packed, after=()):
    wide = sides[0][0][0].shape[1]
    width, hidden = wide - LANES, experts[0][0].shape[2]
    shared_hidden = shared[0][0].shape[1] if shared else 0
    tile, span, ring = shared_hidden or tile_of(hidden, 256), tile_of(width, 1024), 3
    number, pieces_of = len(sides), len(sides[0])
    rows, slots = pieces_of * block, pieces_of * most
    lows = tuple(at * block for side in sides for _, at in side)
    dims = (lows, packed, block, most, width, hidden, shared_hidden, tile, span, ring)
    bf16 = jnp.bfloat16
    vmem, sems = pltpu.VMEM, pltpu.SemaphoreType.DMA
    shared_rows = shared_hidden or 16
    scratch = [
        vmem((number * rows, wide), bf16),
        vmem((2, number * slots, width), bf16),
        vmem((ring, width, tile), bf16),
        vmem((ring, width, tile), bf16),
        vmem((ring, 2, hidden, span), bf16),
        vmem((ring, 2, shared_rows, span), bf16),
        vmem((2, number * slots, hidden), bf16),
        vmem((2, rows, max(shared_rows, LANES)), bf16),
        vmem((number, rows, 2 * slots), bf16),
        vmem((number, width // span, rows, span), bf16),
        sems((number * pieces_of,)),
        sems((2, ring)),
        sems((ring, 2)),
        sems((ring, 2)),
        sems((number, pieces_of, width // span)),
    ]
    token = np.arange(rows)
    before = (token[:, None] < token) & (token[:, None] // block == token // block)
    base = np.broadcast_to(token // block * most, (16, rows))
    before = jnp.asarray(np.concatenate([before, base], axis=0), bf16)
    operands = [part for side in sides for part, _ in side] + [before]
    operands += [part for weights in (*experts, *shared) for part in weights]
    moved = 2 * (sum(part.size for part in operands) + number * rows * width)
    flops = 2 * number * (6 * slots * width * hidden + 4 * rows * slots * width)
    flops += 12 * rows * width * shared_hidden
    operands += after
    operands = [part if part is before else in_hbm(part) for part in operands]
    return pl.pallas_call(
        functools.partial(expert_body, dims),
        out_shape=[pltpu.HBM((block * number, width), bf16)] * pieces_of
        if packed
        else [pltpu.HBM((block, width), bf16)] * (number * pieces_of),
        in_specs=[
            pl.BlockSpec(memory_space=pltpu.VMEM if part is before else pl.ANY) for part in operands
        ],
        out_specs=[pl.BlockSpec(memory_space=pl.ANY)] * (pieces_of * (1 if packed else number)),
        scratch_shapes=scratch,
        compiler_params=pltpu.CompilerParams(vmem_limit_bytes=VMEM_LIMIT),
        cost_estimate=pl.CostEstimate(flops=flops, bytes_accessed=moved, transcendentals=0),
    )(*operands)


def pin(done, moving):
    count = len(done)
    both = lax.optimization_barrier((*done, *moving))
    return list(both[:count]), list(both[count:])


def gather_all(
    tokens, route_ids, route_weight, w_gate, w_up, w_down, shared_gate, shared_up, shared_down
):
    block = tokens.shape[0]
    experts = lax.axis_size("ex") * lax.axis_size("ey")
    most = max(2, 2 * block * route_ids.shape[1] // experts)
    own = with_table(tokens, route_ids, route_weight)
    def right(value):
        return swap(value, "ex", RIGHT)

    def down(value):
        return swap(value, "ex", DOWN)

    def pair(value):
        return swap(value, "ex", PAIR)

    def far(value, mask):
        return swap(value, "ey", mask)

    tie = lax.optimization_barrier
    z2, r0, d0, w_gate_o, w_up_o = far(own, 2), right(own), down(own), pair(w_gate), pair(w_up)
    packed = jnp.concatenate([shared_gate, shared_up], axis=1)
    z2, r0, d0, w_gate_o, w_up_o, w_down_t, packed = tie(
        (z2, r0, d0, w_gate_o, w_up_o, w_down, packed)
    )
    r2, d2, z3, w_down_o = right(z2), down(z2), far(z2, 1), pair(w_down_t)
    r0, r2, d2, z3, w_down_o, packed, shared_down_t, own_t = tie(
        (r0, r2, d2, z3, w_down_o, packed, shared_down, own)
    )
    a2, a0, z1, packed_o, shared_down_o = (
        right(d2), down(r0), far(own_t, 1), pair(packed), pair(shared_down_t)
    )
    a2, a0, z1, packed_o, shared_down_o, z3 = tie((a2, a0, z1, packed_o, shared_down_o, z3))
    experts = [(w_gate, w_up, w_down), (w_gate_o, w_up_o, w_down_o)]
    shared = [(shared_gate, shared_up, shared_down), (packed_o, packed_o, shared_down_o)]
    pair31 = jnp.concatenate([z3, z1], axis=0)
    r31, d31, a31 = right(pair31), down(pair31), far(jnp.concatenate([a2, a0], axis=0), 1)
    sides = [[(own, 0), (r0, 0), (d0, 0), (a0, 0)], [(z2, 0), (r2, 0), (d2, 0), (a2, 0)]]
    out = run_experts(sides, block, most, experts, shared, True)
    out, (r31, d31, a31) = pin(out, (r31, d31, a31))
    sums = out[0]
    from_right, from_down, from_far = right(out[1]), down(out[2]), far(out[3], 1)
    sides = [[(z1, 0), (r31, 1), (d31, 1), (a31, 1)], [(z3, 0), (r31, 0), (d31, 0), (a31, 0)]]
    out = run_experts(sides, block, most, experts, [], False, (sums,))
    out, (from_right, from_down, from_far) = pin(out, (from_right, from_down, from_far))
    sum1, sum3 = out[:4], out[4:]
    across3 = down(add_rows(sum3[3], from_far[block:]))
    across1 = right(add_rows(sum1[3], from_far[:block]))
    hop2 = far(add_rows(sums[block:], from_right[block:], from_down[block:]), 1)
    across3, across1, hop2, plain3, plain1 = tie((across3, across1, hop2, sum3[2], sum1[1]))
    full3, full1 = add_rows(sum3[1], across3), add_rows(sum1[2], across1)
    full3, plain3 = right(full3), down(plain3)
    full3, plain3, full1, plain1 = tie((full3, plain3, full1, plain1))
    full1, plain1 = down(full1), right(plain1)
    part3 = add_rows(sum3[0], plain3, full3, hop2)
    back3 = far(part3, 3)
    part1 = add_rows(sum1[0], plain1, full1)
    back1 = far(part1, 1)
    total = add_rows(sums[:block], from_right[:block], from_down[:block], back3, dtype=jnp.float32)
    return add_rows(total, back1)


def solution(mesh):
    sizes = dict(mesh.shape)

    def shards(*args):
        tokens, route_ids = args[0], args[1]
        slots = max(2, 2 * tokens.shape[0] * route_ids.shape[1] // (sizes["ex"] * sizes["ey"]))
        cube = sizes["ex"] == 2 * DOWN and sizes["ey"] == 4
        if cube and 4 * slots > tokens.shape[0]:
            return gather_all(*args)
        return exchange_slots(*args)

    in_specs = (
        P(("ex", "ey"), None),
        P(("ex", "ey"), None),
        P(("ex", "ey"), None),
        P(("ex", "ey"), None, None),
        P(("ex", "ey"), None, None),
        P(("ex", "ey"), None, None),
        P(None, "ex"),
        P(None, "ex"),
        P("ex", None),
    )
    out_specs = P(("ex", "ey"), None)
    return jax.shard_map(shards, mesh=mesh, in_specs=in_specs, out_specs=out_specs, check_vma=False)
```

```python
import functools

import jax
import jax.numpy as jnp
import numpy as np
from jax import lax
from jax.experimental import pallas as pl
from jax.experimental.pallas import tpu as pltpu
from jax.sharding import PartitionSpec as P


def swiglu(chosen, gate_weight, up_weight, down_weight):
    gate_act = jnp.dot(chosen, gate_weight, preferred_element_type=jnp.float32)
    up_act = jnp.dot(chosen, up_weight, preferred_element_type=jnp.float32)
    hidden = (jax.nn.silu(gate_act) * up_act).astype(jnp.bfloat16)
    return jnp.dot(hidden, down_weight, preferred_element_type=jnp.float32)


def shared_expert(tokens, shared_gate, shared_up, shared_down):
    gathered = lax.all_gather(tokens, "ex", axis=0, tiled=True)
    return lax.psum_scatter(
        swiglu(gathered, shared_gate, shared_up, shared_down).astype(jnp.bfloat16),
        "ex",
        scatter_dimension=0,
        tiled=True,
    ).astype(jnp.float32)


def exchange_slots(
    tokens, route_ids, route_weight, w_gate, w_up, w_down, shared_gate, shared_up, shared_down
):
    tok_rows = tokens.shape[0]
    top_count = route_ids.shape[1]
    width = tokens.shape[1]
    experts = lax.axis_size("ex") * lax.axis_size("ey")
    slot_most = max(2, 2 * tok_rows * top_count // experts)
    capacity = experts * slot_most
    flat_ids = route_ids.reshape(-1)
    onehot = (flat_ids[:, None] == jnp.arange(experts, dtype=jnp.int32)[None, :]).astype(jnp.int32)
    slot_rank = jnp.sum((jnp.cumsum(onehot, axis=0) - onehot) * onehot, axis=1)
    slot_place = flat_ids * slot_most + slot_rank
    matches = (slot_place[:, None] == jnp.arange(capacity, dtype=jnp.int32)[None, :]).astype(
        jnp.float32
    )
    matches = matches.reshape(tok_rows, top_count, capacity)
    placing = jnp.sum(matches, axis=1).astype(jnp.bfloat16)
    combine_mat = jnp.sum(matches * route_weight.astype(jnp.float32)[:, :, None], axis=1).astype(
        jnp.bfloat16
    )
    outgoing = jnp.einsum("tc,td->cd", placing, tokens, preferred_element_type=jnp.float32).astype(
        jnp.bfloat16
    )
    outgoing = outgoing.reshape(experts, slot_most, width)
    arrived = lax.all_to_all(outgoing, ("ex", "ey"), split_axis=0, concat_axis=0, tiled=True)
    layout = arrived.shape
    result = swiglu(arrived.reshape(-1, width), w_gate[0], w_up[0], w_down[0])
    produced = result.astype(jnp.bfloat16).reshape(layout)
    returned = lax.all_to_all(produced, ("ex", "ey"), split_axis=0, concat_axis=0, tiled=True)
    returned = returned.reshape(capacity, width)
    routed = jnp.dot(combine_mat, returned, preferred_element_type=jnp.float32)
    shared = shared_expert(tokens, shared_gate, shared_up, shared_down)
    return (shared + routed).astype(jnp.bfloat16)


PAIR, RIGHT, DOWN = 1, 2, 4
VMEM_LIMIT = 39 * 1024 * 1024


def swap(value, axis, mask):
    size = lax.axis_size(axis)
    return lax.ppermute(value, axis, [(i, i ^ mask) for i in range(size)])


def in_hbm(array):
    return pltpu.with_memory_space_constraint(array, pltpu.HBM)


def add_rows(*parts, dtype=jnp.bfloat16):
    total = parts[0].astype(jnp.float32)
    for part in parts[1:]:
        total = total + part.astype(jnp.float32)
    return total.astype(dtype)


LANES = 128


def tile_of(size, goal):
    return max(t for t in range(LANES, goal + 1, LANES) if size % t == 0)


def table_body(tokens, ids, rates, out):
    top, rows = ids.shape
    width = tokens.shape[1]
    expert = lax.broadcasted_iota(jnp.int32, (LANES, rows), 0)
    table = jnp.zeros((LANES, rows), jnp.float32)
    for k in range(top):
        hit = ids[k : k + 1, :] == expert
        table += jnp.where(hit, rates[k : k + 1, :].astype(jnp.float32), 0.0)
    out[:, :width] = tokens[...]
    out[:, width:] = table.T.astype(out.dtype)


def with_table(tokens, ids, rates):
    rows, width = tokens.shape
    return pl.pallas_call(
        table_body,
        out_shape=jax.ShapeDtypeStruct((rows, width + LANES), tokens.dtype),
    )(tokens, ids.T, rates.T)


def expert_body(dims, *refs):
    lows, packed, block, most, width, hidden, shared_hidden, tile, span, ring = dims
    pieces_of = 4
    sides = len(lows) // pieces_of
    rows = pieces_of * block
    slots = pieces_of * most
    refs = list(refs)

    def take(number):
        out = refs[:number]
        del refs[:number]
        return out

    pieces = take(sides * pieces_of)
    (before_ref,) = take(1)
    experts = [take(3), take(3)]
    shared = [take(3), take(3)] if shared_hidden else []
    outs_of = pieces_of if packed else sides * pieces_of
    take(len(refs) - 15 - outs_of)
    outs = take(outs_of)
    held, chosen, gate, up, down, down_s, act, act_s, back, result = take(10)
    piece_sem, step_sem, span_sem, span_s_sem, out_sem = take(5)
    copy = pltpu.make_async_copy
    f32, bf16 = jnp.float32, jnp.bfloat16

    steps = [(part[0], part[1], low) for part, low in zip(shared, (0, shared_hidden))]
    steps += [
        (part[0].at[0], part[1].at[0], k * tile) for part in experts for k in range(hidden // tile)
    ]
    spans = width // span

    def piece_copy(k):
        rows_of = pl.ds(lows[k], block)
        return copy(pieces[k].at[rows_of], held.at[pl.ds(k * block, block), :], piece_sem.at[k])

    def step_copies(k):
        at = k % ring
        low = steps[k][2]
        gate_low = 0 if k < len(shared) else low
        return [
            copy(steps[k][0].at[:, pl.ds(gate_low, tile)], gate.at[at], step_sem.at[0, at]),
            copy(steps[k][1].at[:, pl.ds(low, tile)], up.at[at], step_sem.at[1, at]),
        ]

    def span_copies(k):
        at = k % ring
        columns = pl.ds(k * span, span)
        both = [
            copy(part[2].at[0, :, columns], down.at[at, e], span_sem.at[at, e])
            for e, part in enumerate(experts)
        ]
        return both + [
            copy(part[2].at[:, columns], down_s.at[at, e], span_s_sem.at[at, e])
            for e, part in enumerate(shared)
        ]

    def out_copy(side, piece, k):
        columns = pl.ds(k * span, span)
        if packed:
            out = outs[piece].at[pl.ds(side * block, block), columns]
        else:
            out = outs[side * pieces_of + piece].at[:, columns]
        rows_of = pl.ds(piece * block, block)
        return copy(result.at[side, k, rows_of, :], out, out_sem.at[side, piece, k])

    def start(copies):
        for one in copies:
            one.start()

    def wait(copies):
        for one in copies:
            one.wait()

    start([piece_copy(k) for k in range(sides * pieces_of)])
    start(step_copies(0))

    ey = lax.axis_size("ey")
    ex = lax.axis_index("ex")
    me = ex * ey + lax.axis_index("ey")
    partner = (ex + PAIR - 2 * PAIR * (ex % (2 * PAIR))) * ey + lax.axis_index("ey")
    row = lax.broadcasted_iota(jnp.int32, (16, LANES), 0)
    lane = lax.broadcasted_iota(jnp.int32, (16, LANES), 1)
    pick = (lane == jnp.where(row == 0, me, partner)).astype(f32).astype(bf16)
    before = before_ref[:rows]
    base = before_ref[rows : rows + 16].astype(f32)[0:1]
    slot = lax.broadcasted_iota(jnp.int32, (slots, rows), 0).astype(f32)
    for side in range(sides):
        wait([piece_copy(k) for k in range(side * pieces_of, (side + 1) * pieces_of)])
        if side == 0:
            for k in range(1, ring):
                start(step_copies(k))
        low = side * rows
        table = held[low : low + rows, width : width + LANES]
        rate = lax.dot_general(
            pick, table, (((1,), (1,)), ((), ())), preferred_element_type=f32
        )
        named = (rate > 0).astype(f32)
        rank = jnp.dot(named.astype(bf16), before, preferred_element_type=f32)
        places = []
        for e in range(2):
            where = jnp.where(named[e : e + 1] > 0, rank[e : e + 1] + base, -1.0)
            place = slot == where
            back[side, :, e * slots : (e + 1) * slots] = jnp.where(
                place, rate[e : e + 1], 0.0
            ).T.astype(bf16)
            places.append(place.astype(f32).astype(bf16))
        picked = jnp.dot(
            jnp.concatenate(places, axis=0),
            held[low : low + rows, :width],
            preferred_element_type=f32,
        ).astype(bf16)
        for e in range(2):
            chosen[e, side * slots : (side + 1) * slots] = picked[e * slots : (e + 1) * slots]

    per = hidden // tile
    for k in range(len(steps)):
        wait(step_copies(k))
        e, at = divmod(k - len(shared), per)
        source = held[:rows, :width] if k < len(shared) else chosen[e]
        g = jnp.dot(source, gate[k % ring], preferred_element_type=f32)
        u = jnp.dot(source, up[k % ring], preferred_element_type=f32)
        h = (jax.nn.silu(g) * u).astype(bf16)
        if k < len(shared):
            act_s[k] = h
        else:
            act[e, :, at * tile : (at + 1) * tile] = h
        if k + ring < len(steps):
            start(step_copies(k + ring))
        elif k + ring - len(steps) < min(ring, spans):
            start(span_copies(k + ring - len(steps)))

    for k in range(spans):
        wait(span_copies(k))
        y = [
            jnp.dot(act[e], down[k % ring, e], preferred_element_type=f32).astype(bf16)
            for e in range(2)
        ]
        for side in range(sides):
            mine = [part[side * slots : (side + 1) * slots] for part in y]
            out = jnp.dot(back[side], jnp.concatenate(mine, axis=0), preferred_element_type=f32)
            if side == 0:
                for e in range(len(shared)):
                    out += jnp.dot(act_s[e], down_s[k % ring, e], preferred_element_type=f32)
            result[side, k] = out.astype(bf16)
            start([out_copy(side, piece, k) for piece in range(pieces_of)])
        if k + ring < spans:
            start(span_copies(k + ring))

    wait(
        [
            out_copy(side, piece, k)
            for side in range(sides)
            for piece in range(pieces_of)
            for k in range(spans)
        ]
    )


def run_experts(sides, block, most, experts, shared, packed, after=()):
    wide = sides[0][0][0].shape[1]
    width, hidden = wide - LANES, experts[0][0].shape[2]
    shared_hidden = shared[0][0].shape[1] if shared else 0
    tile, span, ring = shared_hidden or tile_of(hidden, 256), tile_of(width, 1024), 3
    number, pieces_of = len(sides), len(sides[0])
    rows, slots = pieces_of * block, pieces_of * most
    lows = tuple(at * block for side in sides for _, at in side)
    dims = (lows, packed, block, most, width, hidden, shared_hidden, tile, span, ring)
    bf16 = jnp.bfloat16
    vmem, sems = pltpu.VMEM, pltpu.SemaphoreType.DMA
    shared_rows = shared_hidden or 16
    scratch = [
        vmem((number * rows, wide), bf16),
        vmem((2, number * slots, width), bf16),
        vmem((ring, width, tile), bf16),
        vmem((ring, width, tile), bf16),
        vmem((ring, 2, hidden, span), bf16),
        vmem((ring, 2, shared_rows, span), bf16),
        vmem((2, number * slots, hidden), bf16),
        vmem((2, rows, max(shared_rows, LANES)), bf16),
        vmem((number, rows, 2 * slots), bf16),
        vmem((number, width // span, rows, span), bf16),
        sems((number * pieces_of,)),
        sems((2, ring)),
        sems((ring, 2)),
        sems((ring, 2)),
        sems((number, pieces_of, width // span)),
    ]
    token = np.arange(rows)
    before = (token[:, None] < token) & (token[:, None] // block == token // block)
    base = np.broadcast_to(token // block * most, (16, rows))
    before = jnp.asarray(np.concatenate([before, base], axis=0), bf16)
    operands = [part for side in sides for part, _ in side] + [before]
    operands += [part for weights in (*experts, *shared) for part in weights]
    moved = 2 * (sum(part.size for part in operands) + number * rows * width)
    flops = 2 * number * (6 * slots * width * hidden + 4 * rows * slots * width)
    flops += 12 * rows * width * shared_hidden
    operands += after
    operands = [part if part is before else in_hbm(part) for part in operands]
    return pl.pallas_call(
        functools.partial(expert_body, dims),
        out_shape=[pltpu.HBM((block * number, width), bf16)] * pieces_of
        if packed
        else [pltpu.HBM((block, width), bf16)] * (number * pieces_of),
        in_specs=[
            pl.BlockSpec(memory_space=pltpu.VMEM if part is before else pl.ANY) for part in operands
        ],
        out_specs=[pl.BlockSpec(memory_space=pl.ANY)] * (pieces_of * (1 if packed else number)),
        scratch_shapes=scratch,
        compiler_params=pltpu.CompilerParams(vmem_limit_bytes=VMEM_LIMIT),
        cost_estimate=pl.CostEstimate(flops=flops, bytes_accessed=moved, transcendentals=0),
    )(*operands)


def pin(done, moving):
    count = len(done)
    both = lax.optimization_barrier((*done, *moving))
    return list(both[:count]), list(both[count:])


def gather_all(
    tokens, route_ids, route_weight, w_gate, w_up, w_down, shared_gate, shared_up, shared_down
):
    block = tokens.shape[0]
    experts = lax.axis_size("ex") * lax.axis_size("ey")
    most = max(2, 2 * block * route_ids.shape[1] // experts)
    own = with_table(tokens, route_ids, route_weight)
    def right(value):
        return swap(value, "ex", RIGHT)

    def down(value):
        return swap(value, "ex", DOWN)

    def pair(value):
        return swap(value, "ex", PAIR)

    def far(value, mask):
        return swap(value, "ey", mask)

    tie = lax.optimization_barrier
    z2, r0, d0, w_gate_o, w_up_o = far(own, 2), right(own), down(own), pair(w_gate), pair(w_up)
    packed = jnp.concatenate([shared_gate, shared_up], axis=1)
    z2, r0, d0, w_gate_o, w_up_o, w_down_t, packed = tie(
        (z2, r0, d0, w_gate_o, w_up_o, w_down, packed)
    )
    r2, d2, z3, w_down_o = right(z2), down(z2), far(z2, 1), pair(w_down_t)
    r0, r2, d2, z3, w_down_o, packed, shared_down_t, own_t = tie(
        (r0, r2, d2, z3, w_down_o, packed, shared_down, own)
    )
    a2, a0, z1, packed_o, shared_down_o = (
        right(d2), down(r0), far(own_t, 1), pair(packed), pair(shared_down_t)
    )
    a2, a0, z1, packed_o, shared_down_o, z3 = tie((a2, a0, z1, packed_o, shared_down_o, z3))
    experts = [(w_gate, w_up, w_down), (w_gate_o, w_up_o, w_down_o)]
    shared = [(shared_gate, shared_up, shared_down), (packed_o, packed_o, shared_down_o)]
    pair31 = jnp.concatenate([z3, z1], axis=0)
    r31, d31, a31 = right(pair31), down(pair31), far(jnp.concatenate([a2, a0], axis=0), 1)
    sides = [[(own, 0), (r0, 0), (d0, 0), (a0, 0)], [(z2, 0), (r2, 0), (d2, 0), (a2, 0)]]
    out = run_experts(sides, block, most, experts, shared, True)
    out, (r31, d31, a31) = pin(out, (r31, d31, a31))
    sums = out[0]
    from_right, from_down, from_far = right(out[1]), down(out[2]), far(out[3], 1)
    sides = [[(z1, 0), (r31, 1), (d31, 1), (a31, 1)], [(z3, 0), (r31, 0), (d31, 0), (a31, 0)]]
    out = run_experts(sides, block, most, experts, [], False, (sums,))
    out, (from_right, from_down, from_far) = pin(out, (from_right, from_down, from_far))
    sum1, sum3 = out[:4], out[4:]
    across3 = down(add_rows(sum3[3], from_far[block:]))
    across1 = right(add_rows(sum1[3], from_far[:block]))
    hop2 = far(add_rows(sums[block:], from_right[block:], from_down[block:]), 1)
    across3, across1, hop2, plain3, plain1 = tie((across3, across1, hop2, sum3[2], sum1[1]))
    full3, full1 = add_rows(sum3[1], across3), add_rows(sum1[2], across1)
    full3, plain3 = right(full3), down(plain3)
    full3, plain1 = tie((full3, plain1))
    plain3, full1 = tie((plain3, full1))
    full1, plain1 = down(full1), right(plain1)
    part3 = add_rows(sum3[0], plain3, full3, hop2)
    back3 = far(part3, 3)
    part1 = add_rows(sum1[0], plain1, full1)
    back1 = far(part1, 1)
    total = add_rows(sums[:block], from_right[:block], from_down[:block], back3, dtype=jnp.float32)
    return add_rows(total, back1)


def solution(mesh):
    sizes = dict(mesh.shape)

    def shards(*args):
        tokens, route_ids = args[0], args[1]
        slots = max(2, 2 * tokens.shape[0] * route_ids.shape[1] // (sizes["ex"] * sizes["ey"]))
        cube = sizes["ex"] == 2 * DOWN and sizes["ey"] == 4
        if cube and 4 * slots > tokens.shape[0]:
            return gather_all(*args)
        return exchange_slots(*args)

    in_specs = (
        P(("ex", "ey"), None),
        P(("ex", "ey"), None),
        P(("ex", "ey"), None),
        P(("ex", "ey"), None, None),
        P(("ex", "ey"), None, None),
        P(("ex", "ey"), None, None),
        P(None, "ex"),
        P(None, "ex"),
        P("ex", None),
    )
    out_specs = P(("ex", "ey"), None)
    return jax.shard_map(shards, mesh=mesh, in_specs=in_specs, out_specs=out_specs, check_vma=False)
```
